128 devices in a mesh: ctx: 16 (over y, z_hi, core), exp: 8 (over x, z_lo).
Axes of the slice: x: 4, y: 4, z: 4 (z_hi: 2, z_lo: 2; z = z_hi * 2 + z_lo), core: 2. Of those that a mesh axis runs over, the one named last changes fastest.
Arguments:
- span_q: bfloat16 [2048, 6144], P('ctx', 'exp'), may hold values from -9 to 9
- prompt_kv: bfloat16 [2, 16384, 1024], P(None, 'ctx', 'exp'), may hold values from -10 to 10
- span_kv: bfloat16 [2, 2048, 1024], P(None, 'ctx', 'exp'), may hold values from -10 to 10
- decode_q: bfloat16 [256, 6144], P('ctx', 'exp'), may hold values from -4 to 4
- decode_cache: bfloat16 [2, 256, 256, 1024], P(None, 'ctx', None, 'exp'), may hold values from -10 to 10
- decode_new: bfloat16 [2, 256, 1024], P(None, 'ctx', 'exp'), may hold values from -10.5 to 10.5
- decode_len: int32 [256], P('ctx'), may hold values from 1 to 256, as said below
- residual: bfloat16 [2304, 6144], P('ctx', 'exp'), may hold values from -1.5 to 1.5
- norm_gain: bfloat16 [6144], P('exp'), may hold values from 0.099609375 to 1.8984375
- router: bfloat16 [6144, 8], P('exp'), may hold values from -0.078125 to 0.078125
- expert_ids: int32 [2304, 2], P('ctx'), may hold values from 0 to 7, all different within a row; in each aligned block of 144 rows (0 to 143, 144 to 287, ...) at most 40 rows name the same one
- capacity: int32 [8], replicated, may hold values from 20 to 40, as said below
- w_gate: bfloat16 [8, 6144, 8192], P('exp', None, 'ctx'), may hold values from -0.078125 to 0.078125
- w_up: bfloat16 [8, 6144, 8192], P('exp', None, 'ctx'), may hold values from -0.078125 to 0.078125
- w_down: bfloat16 [8, 8192, 6144], P('exp', 'ctx'), may hold values from -0.0625 to 0.0625
Outputs:
- mixed: bfloat16 [2304, 6144], P('ctx', 'exp')
The draws below stay inside these ranges and needn't reach their ends.
Inputs may be any that keep to these rules, and one draw needn't show every extreme that they name: `decode_len`: some decode row has exactly 256 cached positions. Some expert's capacity is exactly 40. `expert_ids`: in each row block of 144 rows (the rows of one ctx index) no expert is named by more than 40 rows; in some block some expert is named by exactly 40 rows.
All inputs are finite; a program needn't handle non-finite values.
Results may differ from the reference program's by a relative error of at most 0.019.
Values may be sent and summed in bfloat16 or wider, within the bound.
No kernel may reach another device: no remote copies, remote signals or barrier semaphores. Data moves between devices by JAX's collectives and lax.ppermute only.
A program may use at most 192 MiB of HBM per device.

```python
import math
import jax
import jax.numpy as jnp
import numpy as np
from jax import lax

D = 6144
HD = 128
QPK = 6
KVH = 8
EXPERTS = 8
TOPK = 2
FF = 8192
SPAN_DEV = 128
DEC_DEV = 16
DEC_LEN = 256
PROMPT = 16384
SPAN = 2048
DECODE = 256
ROWS_DEV = 144
ROWS = 2304
CAP = 40
FF_DEV = 512
N_CTX = 16


def draw_span_q(key, part):
    key = jax.random.fold_in(key, 5)
    first = jax.random.fold_in(key, 0)
    base = jnp.clip(2.2 * jax.random.normal(first, (SPAN, KVH * QPK, HD), jnp.float32), -9.0, 9.0)
    return base.reshape(SPAN, D).astype(jnp.bfloat16)


def draw_prompt_kv(key, part):
    key = jax.random.fold_in(key, 3)
    base = jnp.clip(jax.random.normal(key, (2, PROMPT, KVH, HD), jnp.float32), -4.0, 4.0)
    return base.reshape(2, PROMPT, KVH * HD).astype(jnp.bfloat16)


def draw_span_kv(key, part):
    key = jax.random.fold_in(key, 29)
    first = jax.random.fold_in(key, 0)
    base = jnp.clip(jax.random.normal(first, (2, SPAN, KVH, HD), jnp.float32), -4.0, 4.0)
    return base.reshape(2, SPAN, KVH * HD).astype(jnp.bfloat16)


def draw_decode_q(key, part):
    key = jax.random.fold_in(key, 17)
    first = jax.random.fold_in(key, 0)
    base = jnp.clip(jax.random.normal(first, (DECODE, KVH * QPK, HD), jnp.float32), -4.0, 4.0)
    return base.reshape(DECODE, D).astype(jnp.bfloat16)


def draw_decode_cache(key, part):
    key = jax.random.fold_in(key, 19)
    base = jnp.clip(jax.random.normal(key, (2, DECODE, DEC_LEN, KVH, HD), jnp.float32), -4.0, 4.0)
    return base.reshape(2, DECODE, DEC_LEN, KVH * HD).astype(jnp.bfloat16)


def draw_decode_new(key, part):
    key = jax.random.fold_in(key, 23)
    base = jnp.clip(jax.random.normal(key, (2, DECODE, KVH, HD), jnp.float32), -4.0, 4.0)
    return base.reshape(2, DECODE, KVH * HD).astype(jnp.bfloat16)


def draw_decode_len(key, part):
    key = jax.random.fold_in(key, 7)
    first, second, third = jax.random.split(key, 3)
    lengths = jnp.minimum(jax.random.randint(first, (DECODE,), 1, DEC_LEN + 1), jax.random.randint(second, (DECODE,), 1, DEC_LEN + 1))
    spot = jax.random.randint(third, (), 0, DECODE)
    return jnp.where(jnp.arange(DECODE) == spot, DEC_LEN, lengths).astype(jnp.int32)


def draw_capacity(key, part):
    key = jax.random.fold_in(key, 11)
    first, second = jax.random.split(key)
    values = jax.random.randint(first, (EXPERTS,), CAP - CAP // 2, CAP + 1)
    spot = jax.random.randint(second, (), 0, EXPERTS)
    return jnp.where(jnp.arange(EXPERTS) == spot, CAP, values).astype(jnp.int32)


def draw_residual(key, part):
    key = jax.random.fold_in(key, 13)
    ramp = jnp.arange(D, dtype=jnp.float32) / D
    values = jnp.clip(jax.random.normal(key, (ROWS, D), jnp.float32), -3.0, 3.0) * jnp.exp(ramp * 1.0986123) * 0.16
    return values.astype(jnp.bfloat16)


def block_levels(key, extent, cuts, low, high):
    def one(dim, blocks):
        heights = jax.random.uniform(jax.random.fold_in(jax.random.fold_in(key, 6), dim), (blocks,), jnp.float32, low / len(cuts), high / len(cuts))
        return jnp.repeat(jnp.exp(heights), extent[dim] // blocks).reshape((-1,) + (1,) * (len(extent) - dim - 1))

    factor_of = one(*cuts[0])
    for cut in cuts[1:]:
        factor_of = factor_of * one(*cut)
    return factor_of


def routed_block(rng, own, number, rows, number_of, top, bound, skew):
    sequence = jax.random.permutation(rng, number_of)
    heavy_load, usual = load_shares(number_of, rows * top, bound, skew, True), load_shares(number_of, rows * top, bound, skew, False)
    places = jnp.arange(number_of)

    def named(tallies, rotation):
        used = int((tallies > 0).sum())
        fixed = max(1, used // 4)
        shifted = fixed + (places - fixed + rotation * (used - fixed)) % max(1, number_of - fixed)
        return jnp.zeros((number_of,), jnp.int32).at[sequence[jnp.where(places < fixed, places, shifted)]].set(jnp.asarray(tallies, jnp.int32))

    tallies = jnp.where(number % 4 == 0, named(heavy_load, number // 4), named(usual, number - number // 4 - 1))
    mixed = jax.random.permutation(jax.random.fold_in(own, 3), number_of)
    donor, sink = mixed[0:number_of // 2 * 2:2], mixed[1:number_of // 2 * 2:2]
    room = jnp.minimum(tallies[donor] - 1, bound - tallies[sink]) // 2
    room = jnp.where((donor == sequence[0]) | (sink == sequence[0]) | (tallies[sink] == 0), 0, jnp.maximum(room, 0))
    shifted = jax.random.randint(jax.random.fold_in(own, 4), (number_of // 2,), 0, 1 << 20) % (room + 1)
    tallies = tallies.at[donor].add(-shifted).at[sink].add(shifted)
    labels = jnp.searchsorted(jnp.cumsum(tallies), jnp.arange(rows * top), side="right").astype(jnp.int32)
    listing = labels.reshape(top, rows).T
    listing = listing[jax.random.permutation(jax.random.fold_in(own, 1), rows)]
    rotation = jax.random.randint(jax.random.fold_in(own, 2), (rows, 1), 0, top)
    return jnp.take_along_axis(listing, (jnp.arange(top)[None, :] + rotation) % top, axis=1)


def load_shares(amount, total, reach, slope, full):
    portions = [(1 << 20) // math.isqrt(standing ** slope) + 1 for standing in range(1, amount + 1)]
    largest = reach if full else min(reach, max(-(-total // amount), total * portions[0] // sum(portions)))
    least = 1 if total - largest >= amount - 1 else 0
    counts, spare = [largest] + [least] * (amount - 1), total - largest - least * (amount - 1)
    while spare > 0:
        candidates = [i for i in range(1, amount) if counts[i] < largest] or [i for i in range(1, amount) if counts[i] < reach]
        whole, left = sum([portions[i] for i in candidates]), spare
        for i in candidates:
            extra = min(reach - counts[i], max(1, left * portions[i] // whole), spare)
            counts[i] = counts[i] + extra
            spare = spare - extra
    return np.array(counts)


def normal_values(rng, extent, width, bound, shards=(), kind=jnp.bfloat16):
    values = jax.random.normal(rng, extent, jnp.float32) * width
    if len(shards) > 0:
        values = block_levels(rng, extent, shards, -0.22, 0.18) * values
    return jnp.clip(values, min=-bound, max=bound).astype(kind)


def setup_inputs(seed: int = 0) -> dict:
    key_of = jax.random.split(jax.random.key(seed), 16)
    span_q = draw_span_q(jax.random.fold_in(key_of[15], 71), 0)
    prompt_kv = draw_prompt_kv(jax.random.fold_in(key_of[15], 71), 0)
    span_kv = draw_span_kv(jax.random.fold_in(key_of[15], 71), 0)
    decode_q = draw_decode_q(jax.random.fold_in(key_of[15], 71), 0)
    decode_cache = draw_decode_cache(jax.random.fold_in(key_of[15], 71), 0)
    decode_new = draw_decode_new(jax.random.fold_in(key_of[15], 71), 0)
    decode_len = draw_decode_len(jax.random.fold_in(key_of[15], 71), 0)
    residual = draw_residual(jax.random.fold_in(key_of[15], 71), 0)
    norm_gain = jnp.clip(1.0 + 0.18 * jax.random.normal(key_of[8], (D,), jnp.float32), 0.099609375, 1.8984375).astype(jnp.bfloat16)
    router = normal_values(key_of[9], (D, EXPERTS), D ** -0.5, 0.078125, ((0, 8),))
    expert_ids_keys = jax.random.split(jax.random.fold_in(key_of[10], 1), ROWS // ROWS_DEV)
    expert_ids_turns = jax.random.permutation(jax.random.fold_in(key_of[10], 3), ROWS // ROWS_DEV)
    expert_ids = jax.vmap(lambda own, number: routed_block(jax.random.fold_in(key_of[10], 2), own, number, ROWS_DEV, EXPERTS, TOPK, CAP, 2))(expert_ids_keys, expert_ids_turns).reshape((ROWS, TOPK))
    capacity = draw_capacity(jax.random.fold_in(key_of[15], 71), 0)
    w_gate = normal_values(key_of[12], (EXPERTS, D, FF), D ** -0.5, 0.078125, ((0, 8), (2, 16)))
    w_up = normal_values(key_of[13], (EXPERTS, D, FF), D ** -0.5, 0.078125, ((0, 8), (2, 16)))
    w_down = normal_values(key_of[14], (EXPERTS, FF, D), FF ** -0.5, 0.0625, ((0, 8), (1, 16)))
    return {"span_q": span_q, "prompt_kv": prompt_kv, "span_kv": span_kv, "decode_q": decode_q, "decode_cache": decode_cache, "decode_new": decode_new, "decode_len": decode_len, "residual": residual, "norm_gain": norm_gain, "router": router, "expert_ids": expert_ids, "capacity": capacity, "w_gate": w_gate, "w_up": w_up, "w_down": w_down}


NEG = -1e+30
EPS = 1e-05

def span_attention(span_q, prompt_kv, span_kv):
    total_keys = PROMPT + SPAN
    keys = jnp.concatenate([prompt_kv[0], span_kv[0]], axis=0).reshape(total_keys, KVH, HD)
    values = jnp.concatenate([prompt_kv[1], span_kv[1]], axis=0).reshape(total_keys, KVH, HD)
    queries = span_q.reshape(SPAN, KVH, QPK, HD)
    key_place = jnp.arange(total_keys, dtype=jnp.int32) - PROMPT
    block = math.gcd(SPAN, 512)
    starts = jnp.arange(SPAN // block, dtype=jnp.int32) * block
    keys_t = jnp.transpose(keys, (1, 0, 2))
    values_t = jnp.transpose(values, (1, 0, 2))
    queries_t = jnp.transpose(queries, (1, 0, 2, 3))

    def one_head(operands):
        head_q, head_k, head_v = operands
        key_float = head_k.astype(jnp.float32)
        value_float = head_v.astype(jnp.float32)

        def one_block(start):
            query_block = lax.dynamic_slice_in_dim(head_q, start, block, 0).astype(jnp.float32)
            scores = jnp.einsum('cqd,kd->cqk', query_block, key_float) * HD ** (-0.5)
            place = start + jnp.arange(block, dtype=jnp.int32)
            visible = (key_place[None, :] <= place[:, None])[:, None, :]
            top = lax.optimization_barrier(jnp.max(jnp.where(visible, scores, NEG), axis=-1, keepdims=True))
            weights = jnp.where(visible, jnp.exp(scores - top), 0.0)
            probs = lax.optimization_barrier(weights.astype(jnp.bfloat16)).astype(jnp.float32)
            summed = jnp.einsum('cqk,kd->cqd', probs, value_float)
            return summed / lax.optimization_barrier(jnp.sum(weights, axis=-1, keepdims=True))
        return lax.map(one_block, starts)
    result = lax.map(one_head, (queries_t, keys_t, values_t))
    result = result.reshape(KVH, SPAN, QPK, HD).transpose(1, 0, 2, 3).reshape(SPAN, D)
    return result.astype(jnp.bfloat16)

def decode_attention(decode_q, decode_cache, decode_new, decode_len):
    queries = decode_q.reshape(DECODE, KVH, QPK, HD).astype(jnp.float32)
    keys = decode_cache[0].reshape(DECODE, DEC_LEN, KVH, HD).astype(jnp.float32)
    values = decode_cache[1].reshape(DECODE, DEC_LEN, KVH, HD).astype(jnp.float32)
    own_key = decode_new[0].reshape(DECODE, KVH, HD).astype(jnp.float32)
    own_value = decode_new[1].reshape(DECODE, KVH, HD).astype(jnp.float32)
    scale = HD ** (-0.5)
    scores = jnp.einsum('rgqd,rlgd->rgql', queries, keys) * scale
    live = (jnp.arange(DEC_LEN, dtype=jnp.int32)[None, :] < decode_len[:, None])[:, None, None, :]
    own = jnp.einsum('rgqd,rgd->rgq', queries, own_key) * scale
    top = jnp.maximum(lax.optimization_barrier(jnp.max(jnp.where(live, scores, NEG), axis=-1)), own)
    weights = jnp.where(live, jnp.exp(scores - top[..., None]), 0.0)
    own_weight = jnp.exp(own - top)
    probs = lax.optimization_barrier(weights.astype(jnp.bfloat16)).astype(jnp.float32)
    own_prob = lax.optimization_barrier(own_weight.astype(jnp.bfloat16)).astype(jnp.float32)
    summed = jnp.einsum('rgql,rlgd->rgqd', probs, values) + own_prob[..., None] * own_value[:, :, None, :]
    result = summed / (lax.optimization_barrier(jnp.sum(weights, axis=-1)) + own_weight)[..., None]
    return result.reshape(DECODE, D).astype(jnp.bfloat16)

def experts(normed, route_weight, expert_ids, capacity, w_gate, w_up, w_down):
    assigns = ROWS_DEV * TOPK
    slots = CAP * EXPERTS
    ids = expert_ids.reshape(N_CTX, assigns)
    onehot = (ids[:, :, None] == jnp.arange(EXPERTS, dtype=jnp.int32)[None, None, :]).astype(jnp.int32)
    prior = jnp.cumsum(onehot, axis=1) - onehot
    position = lax.optimization_barrier(jnp.sum(prior * onehot, axis=-1))
    limit = lax.optimization_barrier(jnp.sum(onehot * capacity[None, None, :], axis=-1))
    kept = position < limit
    slot = position * EXPERTS + ids
    select = kept[:, :, None] & (slot[:, :, None] == jnp.arange(slots, dtype=jnp.int32)[None, None, :])
    select = select.astype(jnp.float32).reshape(N_CTX, ROWS_DEV, TOPK, slots)
    rows = lax.optimization_barrier(normed).astype(jnp.float32).reshape(N_CTX, ROWS_DEV, D)
    placed = jnp.einsum('crs,crd->csd', lax.optimization_barrier(jnp.sum(select, axis=2)), rows).astype(jnp.bfloat16)
    by_expert = placed.reshape(N_CTX, CAP, EXPERTS, D).transpose(2, 0, 1, 3).reshape(EXPERTS, N_CTX * CAP, D)

    def one_expert(operands):
        inputs, gate_w, up_w, down_w = operands
        gate = jnp.dot(inputs, gate_w, preferred_element_type=jnp.float32)
        up = jnp.dot(inputs, up_w, preferred_element_type=jnp.float32)
        hidden = (jax.nn.silu(gate) * up).astype(jnp.bfloat16)
        pieces = hidden.reshape(N_CTX * CAP, N_CTX, FF_DEV).transpose(1, 0, 2)
        downs = down_w.reshape(N_CTX, FF_DEV, D)

        def add_piece(total, operand):
            piece, down_piece = operand
            part = jnp.dot(piece, down_piece, preferred_element_type=jnp.float32).astype(jnp.bfloat16)
            return (total + lax.optimization_barrier(part).astype(jnp.float32), None)
        total, unused = lax.scan(add_piece, jnp.zeros((N_CTX * CAP, D), jnp.float32), (pieces, downs))
        return total.astype(jnp.bfloat16)
    outputs = lax.map(one_expert, (by_expert, w_gate, w_up, w_down))
    back = outputs.reshape(EXPERTS, N_CTX, CAP, D).transpose(1, 2, 0, 3).reshape(N_CTX, slots, D)
    back = lax.optimization_barrier(back).astype(jnp.float32)
    mixing = lax.optimization_barrier(jnp.sum(select * route_weight.reshape(N_CTX, ROWS_DEV, TOPK)[..., None], axis=2))
    moe = jnp.einsum('crs,csd->crd', mixing, back, precision=lax.Precision.HIGHEST)
    return moe.reshape(ROWS, D)

def reference(span_q, prompt_kv, span_kv, decode_q, decode_cache, decode_new, decode_len, residual, norm_gain, router, expert_ids, capacity, w_gate, w_up, w_down):
    span_out = span_attention(span_q, prompt_kv, span_kv)
    decode_out = decode_attention(decode_q, decode_cache, decode_new, decode_len)
    attn = jnp.concatenate([span_out.reshape(N_CTX, SPAN_DEV, D), decode_out.reshape(N_CTX, DEC_DEV, D)], axis=1).reshape(ROWS, D)
    carried = residual.astype(jnp.float32) + lax.optimization_barrier(attn).astype(jnp.float32)
    rscale = lax.rsqrt(lax.optimization_barrier(jnp.sum(carried * carried, axis=1)) / D + EPS)
    gained = carried * norm_gain.astype(jnp.float32)
    logits = jnp.dot(gained, router.astype(jnp.float32), precision=lax.Precision.HIGHEST) * rscale[:, None]
    normed = (gained * rscale[:, None]).astype(jnp.bfloat16)
    onehot = expert_ids[:, :, None] == jnp.arange(EXPERTS, dtype=jnp.int32)[None, None, :]
    chosen = lax.optimization_barrier(jnp.sum(jnp.where(onehot, logits[:, None, :], 0.0), axis=-1))
    route_weight = jax.nn.sigmoid(chosen - chosen[:, ::-1])
    moe = experts(normed, route_weight, expert_ids, capacity, w_gate, w_up, w_down)
    return (carried + moe).astype(jnp.bfloat16)
```

```python
import functools

import jax
import jax.numpy as jnp
from jax import lax
from jax.experimental import pallas as pl
from jax.experimental.pallas import tpu as pltpu
from jax.sharding import PartitionSpec as P

D = 6144
HD = 128
QPK = 6
EXPERTS = 8
TOPK = 2
CAP = 40
FF_DEV = 512
SPAN_DEV = 128
ROWS_DEV = 144
N_Y = 4
WIDTH = D // EXPERTS
SLOTS = CAP * EXPERTS
MSG = QPK * HD + 128
EXTRA = 8

F1 = 4096
F2 = D - F1

NEG = -1e30
EPS = 1e-05
LOG2E = 1.4426950408889634
SCALE2 = HD ** (-0.5) * LOG2E
BF16 = jnp.bfloat16
F32 = jnp.float32
MIB = 2**20
VMEM = pl.BlockSpec(memory_space=pltpu.VMEM)
SMEM = pl.BlockSpec(memory_space=pltpu.SMEM)


def ctx_index(y, z, core):
    return y * 4 + z * 2 + core


def moved(value, place):
    pairs = []
    for y in range(N_Y):
        for z in range(2):
            for core in range(2):
                pairs.append((ctx_index(y, z, core), ctx_index(*place(y, z, core))))
    return lax.ppermute(value, "ctx", pairs)


def along_y(value, steps):
    return moved(value, lambda y, z, core: ((y + steps) % N_Y, z, core))


def across_z(value):
    return moved(value, lambda y, z, core: (y, 1 - z, core))


def across_core(value):
    return moved(value, lambda y, z, core: (y, z, 1 - core))


def dot_nt(a, b, precision=None):
    return lax.dot_general(
        a, b, (((1,), (1,)), ((), ())), preferred_element_type=F32, precision=precision
    )


def head_weights(query, keys, span_keys, place, h):
    scores = dot_nt(query, keys)
    span = dot_nt(query, span_keys)
    row = lax.broadcasted_iota(jnp.int32, span.shape, 0) + place[0] * SPAN_DEV
    col = lax.broadcasted_iota(jnp.int32, span.shape, 1)
    where = jnp.where(
        col < SPAN_DEV, place[1] * SPAN_DEV + col, (place[2] - 1) * SPAN_DEV + col
    )
    span = jnp.where(where <= row, span, NEG)
    top = jnp.maximum(
        jnp.max(scores, axis=1, keepdims=True), jnp.max(span, axis=1, keepdims=True)
    )
    return (
        top,
        jnp.exp2((scores - top) * SCALE2).astype(BF16),
        jnp.exp2((span - top) * SCALE2).astype(BF16),
    )


def read_blocks(a_ref, b_ref):
    span = SPAN_DEV
    prompt = a_ref.shape[1] - span
    keys = jnp.concatenate([a_ref[0, :prompt, :], b_ref[0, :prompt, :]], axis=0)
    span_keys = jnp.concatenate([a_ref[0, prompt:, :], b_ref[0, prompt:, :]], axis=0)
    values = jnp.concatenate([a_ref[1, :prompt, :], b_ref[1, :prompt, :]], axis=0)
    span_values = jnp.concatenate([a_ref[1, prompt:, :], b_ref[1, prompt:, :]], axis=0)
    values = jnp.concatenate([values, jnp.ones(values.shape, BF16)], axis=1)
    span_values = jnp.concatenate([span_values, jnp.ones(span_values.shape, BF16)], axis=1)
    return keys, span_keys, values, span_values


def flash_first(place_ref, q_ref, a_ref, b_ref, sum_ref, total_ref, top_ref):
    keys, span_keys, values, span_values = read_blocks(a_ref, b_ref)
    place = (place_ref[0], place_ref[1], place_ref[2])
    for h in range(QPK):
        lanes = slice(h * HD, (h + 1) * HD)
        top, probs, span_probs = head_weights(q_ref[:, lanes], keys, span_keys, place, h)
        out = jnp.dot(probs, values, preferred_element_type=F32)
        out = out + jnp.dot(span_probs, span_values, preferred_element_type=F32)
        sum_ref[:, lanes] = out[:, :HD]
        total_ref[:, lanes] = out[:, HD:]
        top_ref[:, lanes] = jnp.broadcast_to(top, (SPAN_DEV, HD))


def split3(value):
    hi = value.astype(BF16).astype(F32)
    rest = value - hi
    mid = rest.astype(BF16).astype(F32)
    return hi, mid, rest - mid


def flash_last(place_ref, q_ref, a_ref, b_ref, sum_ref, total_ref, top_ref, msg_ref):
    keys, span_keys, values, span_values = read_blocks(a_ref, b_ref)
    place = (place_ref[0], place_ref[1], place_ref[2])
    lane = lax.broadcasted_iota(jnp.int32, (SPAN_DEV, 128), 1)
    stats = jnp.zeros((SPAN_DEV, 128), F32)
    for h in range(QPK):
        lanes = slice(h * HD, (h + 1) * HD)
        top, probs, span_probs = head_weights(q_ref[:, lanes], keys, span_keys, place, h)
        out = jnp.dot(probs, values, preferred_element_type=F32)
        out = out + jnp.dot(span_probs, span_values, preferred_element_type=F32)
        before = top_ref[:, lanes]
        newest = jnp.maximum(before, top)
        old = jnp.exp2((before - newest) * SCALE2)
        new = jnp.exp2((top - newest) * SCALE2)
        total = total_ref[:, lanes] * old + out[:, HD:] * new
        summed = sum_ref[:, lanes] * old + out[:, :HD] * new
        msg_ref[:, lanes] = (summed / total).astype(BF16)
        for i, part in enumerate(split3(newest * SCALE2 + jnp.log2(total))):
            stats = jnp.where(lane == 3 * h + i, part, stats)
    msg_ref[:, QPK * HD :] = stats.astype(BF16)


FLASH_COST = pl.CostEstimate(
    flops=4 * 768 * 2304 * 128, bytes_accessed=4 * MIB, transcendentals=768 * 2304
)


def flash_start(place, queries, block_a, block_b):
    shape = jax.ShapeDtypeStruct((SPAN_DEV, QPK * HD), F32)
    return pl.pallas_call(
        flash_first,
        out_shape=(shape,) * 3,
        in_specs=[SMEM, VMEM, VMEM, VMEM],
        out_specs=(VMEM,) * 3,
        compiler_params=pltpu.CompilerParams(vmem_limit_bytes=32 * MIB),
        cost_estimate=FLASH_COST,
        name="flash_first",
    )(place, queries, block_a, block_b)


def flash_end(place, queries, block_a, block_b, state):
    return pl.pallas_call(
        flash_last,
        out_shape=jax.ShapeDtypeStruct((SPAN_DEV, MSG), BF16),
        in_specs=[SMEM] + [VMEM] * 6,
        out_specs=VMEM,
        compiler_params=pltpu.CompilerParams(vmem_limit_bytes=32 * MIB),
        cost_estimate=FLASH_COST,
        name="flash_last",
    )(place, queries, block_a, block_b, *state)


def dispatch_kernel(
    m0, m1, m2, m3, decode_ref, residual_ref, gain_ref, router_ref, placing_ref, carried_ref, out_ref
):
    msgs = (m0, m1, m2, m3)
    for h in range(QPK):
        lanes = slice(h * HD, (h + 1) * HD)
        levels = []
        for m in msgs:
            at = QPK * HD + 3 * h
            stat = m[:, at : at + 3].astype(F32)
            levels.append(stat[:, 0:1] + stat[:, 1:2] + stat[:, 2:3])
        top = functools.reduce(jnp.maximum, levels)
        weights = [jnp.exp2(level - top) for level in levels]
        total = sum(weights)
        summed = sum(w * m[:, lanes].astype(F32) for w, m in zip(weights, msgs))
        attn = (summed / total).astype(BF16).astype(F32)
        carried_ref[:SPAN_DEV, lanes] = residual_ref[:SPAN_DEV, lanes].astype(F32) + attn
    carried_ref[SPAN_DEV:, :] = residual_ref[SPAN_DEV:, :].astype(F32) + decode_ref[...].astype(F32)
    carried = carried_ref[...]
    gained = carried * gain_ref[...].astype(F32)
    logits = dot_nt(router_ref[...].astype(F32), gained, lax.Precision.HIGHEST)
    squares = dot_nt(jnp.ones((EXTRA, WIDTH), F32), carried * carried, lax.Precision.HIGHEST)
    log_hi, log_mid, _ = split3(logits)
    sq_hi, sq_mid, _ = split3(squares)
    row = lax.broadcasted_iota(jnp.int32, squares.shape, 0)
    sq = jnp.where(row == 0, sq_hi, sq_mid)
    placed = jnp.dot(placing_ref[...], gained.astype(BF16), preferred_element_type=F32).astype(BF16)
    for e in range(EXPERTS):
        out_ref[e, :CAP, :] = placed[e * CAP : (e + 1) * CAP, :]
        out_ref[e, CAP:, :] = jnp.zeros((EXTRA, WIDTH), BF16)
        out_ref[e, CAP:, 0:ROWS_DEV] = log_hi.astype(BF16)
        out_ref[e, CAP:, 256 : 256 + ROWS_DEV] = log_mid.astype(BF16)
        out_ref[e, CAP:, 512 : 512 + ROWS_DEV] = sq.astype(BF16)


def arrive_kernel(got_ref, placing_ref, first_ref, second_ref, logits_ref):
    stats = got_ref[0, CAP:, :].astype(F32)
    for e in range(1, EXPERTS):
        stats = stats + got_ref[e, CAP:, :].astype(F32)
    logits = stats[:, 0:ROWS_DEV] + stats[:, 256 : 256 + ROWS_DEV]
    squares = stats[0:1, 512 : 512 + ROWS_DEV] + stats[1:2, 512 : 512 + ROWS_DEV]
    rscale = lax.rsqrt(squares / D + EPS)
    logits_ref[...] = logits * rscale
    scale = jnp.sum(placing_ref[...].astype(F32) * rscale, axis=1, keepdims=True)
    for e in range(EXPERTS):
        rows = (got_ref[e, :CAP, :].astype(F32) * scale).astype(BF16)
        begin = e * WIDTH
        end = begin + WIDTH
        if end <= F1:
            first_ref[:, begin:end] = rows
        elif begin >= F1:
            second_ref[:, begin - F1 : end - F1] = rows
        else:
            first_ref[:, begin:F1] = rows[:, : F1 - begin]
            second_ref[:, : end - F1] = rows[:, F1 - begin :]


def expert_inputs(pieces, x_ref):
    for ref, row, col in pieces:
        rows, cols = ref.shape
        x_ref[row : row + rows, col : col + cols] = ref[...]


def gate_first(layout, n_pieces, *refs):
    pieces = refs[:n_pieces]
    g_own, g_other, u_own, u_other, gate_ref, up_ref, x_ref = refs[n_pieces:]
    step = pl.program_id(0)

    @pl.when(step == 0)
    def _():
        expert_inputs([(r, *at) for r, at in zip(pieces, layout)], x_ref)

    @pl.when(step < 2)
    def _():
        gate_ref[...] = jnp.dot(x_ref[...], g_own[0], preferred_element_type=F32)
        up_ref[...] = jnp.dot(x_ref[...], u_own[0], preferred_element_type=F32)

    @pl.when(step >= 2)
    def _():
        gate_ref[...] = jnp.dot(x_ref[...], g_other[0], preferred_element_type=F32)
        up_ref[...] = jnp.dot(x_ref[...], u_other[0], preferred_element_type=F32)


def gate_last(layout, n_pieces, *refs):
    pieces = refs[:n_pieces]
    gate_ref, up_ref, g_own, g_other, u_own, u_other, hidden_ref, x_ref = refs[n_pieces:]
    step = pl.program_id(0)

    @pl.when(step == 0)
    def _():
        expert_inputs([(r, *at) for r, at in zip(pieces, layout)], x_ref)

    def finish(g, u):
        gate = gate_ref[...] + jnp.dot(x_ref[...], g, preferred_element_type=F32)
        up = up_ref[...] + jnp.dot(x_ref[...], u, preferred_element_type=F32)
        hidden_ref[...] = (gate / (1.0 + jnp.exp(-gate)) * up).astype(BF16)

    @pl.when(step < 2)
    def _():
        finish(g_own[0], u_own[0])

    @pl.when(step >= 2)
    def _():
        finish(g_other[0], u_other[0])


N_TILE = 256


def gate_specs(first, depth):
    own = pl.BlockSpec((1, depth, N_TILE), lambda n: (0, first, jnp.minimum(n, 1)))
    other = pl.BlockSpec((1, depth, N_TILE), lambda n: (0, first, jnp.maximum(n - 2, 0)))
    return [own, other, own, other]


def gate_call(kernel, pieces, layout, state, weights, first, depth, outs, dtype):
    whole = [pl.BlockSpec(p.shape, lambda n: (0, 0)) for p in pieces]
    tile = pl.BlockSpec((SLOTS, N_TILE), lambda n: (0, n))
    shape = jax.ShapeDtypeStruct((SLOTS, 2 * FF_DEV), dtype)
    return pl.pallas_call(
        functools.partial(kernel, layout, len(pieces)),
        grid=(2 * FF_DEV // N_TILE,),
        out_shape=(shape,) * outs,
        in_specs=whole + [tile] * len(state) + gate_specs(first, depth),
        out_specs=(tile,) * outs,
        scratch_shapes=[pltpu.VMEM((SLOTS, depth), BF16)],
        compiler_params=pltpu.CompilerParams(vmem_limit_bytes=48 * MIB),
        cost_estimate=pl.CostEstimate(
            flops=2 * SLOTS * depth * 4 * FF_DEV,
            bytes_accessed=depth * 4 * FF_DEV * 2,
            transcendentals=0,
        ),
        name=kernel.__name__,
    )(*pieces, *state, *weights)


def down_kernel(hidden_ref, own_ref, other_ref, out_ref):
    out = jnp.dot(hidden_ref[:, :FF_DEV], own_ref[0], preferred_element_type=F32)
    out = out + jnp.dot(hidden_ref[:, FF_DEV:], other_ref[0], preferred_element_type=F32)
    out_ref[...] = out.astype(BF16)


def down_call(hidden, own, other, first, width, tile):
    count = width // tile
    begin = first // tile
    weight = pl.BlockSpec((1, FF_DEV, tile), lambda n: (0, 0, begin + n))
    return pl.pallas_call(
        down_kernel,
        grid=(count,),
        out_shape=jax.ShapeDtypeStruct((SLOTS, width), BF16),
        in_specs=[pl.BlockSpec(hidden.shape, lambda n: (0, 0)), weight, weight],
        out_specs=pl.BlockSpec((SLOTS, tile), lambda n: (0, n)),
        compiler_params=pltpu.CompilerParams(vmem_limit_bytes=40 * MIB),
        cost_estimate=pl.CostEstimate(
            flops=2 * SLOTS * width * 2 * FF_DEV,
            bytes_accessed=width * 2 * FF_DEV * 2,
            transcendentals=0,
        ),
        name="down",
    )(hidden, own, other)


def final_kernel(hi_ref, lo_ref, got_ref, carried_ref, out_ref):
    got = got_ref[...]
    moe = jnp.dot(hi_ref[...], got, preferred_element_type=F32)
    moe = moe + jnp.dot(lo_ref[...], got, preferred_element_type=F32)
    out_ref[...] = (carried_ref[...] + moe).astype(BF16)


def mixing_kernel(slot_ref, weight_ref, hi_ref, lo_ref):
    lane = lax.broadcasted_iota(jnp.int32, (ROWS_DEV, SLOTS), 1)
    mix = jnp.zeros((ROWS_DEV, SLOTS), F32)
    for k in range(TOPK):
        mix = jnp.where(slot_ref[:, k : k + 1] == lane, weight_ref[:, k : k + 1], mix)
    hi = mix.astype(BF16)
    hi_ref[...] = hi
    lo_ref[...] = (mix - hi.astype(F32)).astype(BF16)


def decode_block(decode_q, decode_cache, decode_new, decode_len):
    rows = decode_q.shape[0]
    length = decode_cache.shape[2]
    queries = decode_q.reshape(rows, QPK, HD)
    keys = decode_cache[0]
    values = decode_cache[1]
    own_key = decode_new[0]
    own_value = decode_new[1]
    scale = HD ** (-0.5)
    scores = jnp.einsum("rqd,rld->rql", queries, keys, preferred_element_type=F32) * scale
    live = (jnp.arange(length, dtype=jnp.int32)[None, :] < decode_len[:, None])[:, None, :]
    own = jnp.einsum("rqd,rd->rq", queries, own_key, preferred_element_type=F32) * scale
    top = jnp.maximum(jnp.max(jnp.where(live, scores, NEG), axis=-1), own)
    weights = jnp.where(live, jnp.exp(scores - top[..., None]), 0.0)
    own_weight = jnp.exp(own - top)
    own_prob = lax.optimization_barrier(own_weight.astype(BF16)).astype(F32)
    summed = jnp.einsum("rql,rld->rqd", weights.astype(BF16), values, preferred_element_type=F32)
    summed = summed + own_prob[..., None] * own_value.astype(F32)[:, None, :]
    result = summed / (jnp.sum(weights, axis=-1) + own_weight)[..., None]
    return result.reshape(rows, QPK * HD).astype(BF16)


def add(*values):
    return functools.reduce(jnp.add, [v.astype(F32) for v in values]).astype(BF16)


def scatter_y(own, left, right, far):
    half = far.shape[1] // 2
    from_left = along_y(far[:, :half], 1)
    from_right = along_y(far[:, half:], -1)
    right = jnp.concatenate([add(right[:, :half], from_left), right[:, half:]], axis=1)
    left = jnp.concatenate([left[:, :half], add(left[:, half:], from_right)], axis=1)
    return own, along_y(right, 1), along_y(left, -1)


def on_device(
    span_q,
    prompt_kv,
    span_kv,
    decode_q,
    decode_cache,
    decode_new,
    decode_len,
    residual,
    norm_gain,
    router,
    expert_ids,
    capacity,
    w_gate,
    w_up,
    w_down,
):
    here = lax.axis_index("ctx")
    y, z, core = here // 4, (here // 2) % 2, here % 2
    kv = jnp.concatenate([prompt_kv, span_kv], axis=1)
    kv_core = across_core(kv)
    kv_z = across_z(kv)
    q_left, q_right, q_far = along_y(span_q, 1), along_y(span_q, -1), along_y(span_q, 2)
    kv_zc = across_core(kv_z)
    near = (kv, kv_core, ctx_index(0, z, core), ctx_index(0, z, 1 - core))
    other = (kv_z, kv_zc, ctx_index(0, 1 - z, core), ctx_index(0, 1 - z, 1 - core))

    def place_of(steps, blocks):
        source = ctx_index((y + steps) % N_Y, z, core)
        return jnp.stack([source, y * 4 + blocks[2], y * 4 + blocks[3]]).astype(jnp.int32)

    queries = {0: span_q, -1: q_left, 1: q_right, 2: q_far}
    state = {}
    for steps in (0, -1, 1, 2):
        state[steps] = flash_start(place_of(steps, near), queries[steps], near[0], near[1])
    msg = {}
    for steps in (2, -1, 1, 0):
        msg[steps] = flash_end(
            place_of(steps, other), queries[steps], other[0], other[1], state[steps]
        )
    msg_far = along_y(msg[2], 2)
    msg_left = along_y(msg[1], 1)
    msg_right = along_y(msg[-1], -1)

    gate_own, up_own, down_own, kv_zc = lax.optimization_barrier((w_gate, w_up, w_down, kv_zc))
    gate_other = across_core(gate_own)
    up_other = across_core(up_own)
    down_other = across_core(down_own)

    expert_range = jnp.arange(EXPERTS, dtype=jnp.int32)
    flat_ids = expert_ids.reshape(ROWS_DEV * TOPK)
    assign = (flat_ids[:, None] == expert_range[None, :]).astype(jnp.int32)
    prior = jnp.cumsum(assign, axis=0) - assign
    position = jnp.sum(prior * assign, axis=1)
    limit = jnp.sum(assign * capacity[None, :], axis=1)
    slot = jnp.where(position < limit, flat_ids * CAP + position, -1).reshape(ROWS_DEV, TOPK)
    slot_range = jnp.arange(SLOTS, dtype=jnp.int32)[:, None]
    placing = ((slot[:, 0][None, :] == slot_range) | (slot[:, 1][None, :] == slot_range)).astype(
        BF16
    )
    own_placing = lax.dynamic_slice_in_dim(placing, lax.axis_index("exp") * CAP, CAP, 0)

    decode_out = decode_block(decode_q, decode_cache, decode_new, decode_len)
    carried, outgoing = pl.pallas_call(
        dispatch_kernel,
        out_shape=(
            jax.ShapeDtypeStruct((ROWS_DEV, WIDTH), F32),
            jax.ShapeDtypeStruct((EXPERTS, CAP + EXTRA, WIDTH), BF16),
        ),
        in_specs=[VMEM] * 9,
        out_specs=(VMEM, VMEM),
        name="dispatch",
    )(
        msg[0],
        msg_far,
        msg_left,
        msg_right,
        decode_out,
        residual,
        norm_gain.reshape(1, WIDTH),
        router.T,
        placing,
    )
    got = lax.all_to_all(outgoing, "exp", split_axis=0, concat_axis=0, tiled=True)
    first, second, logits = pl.pallas_call(
        arrive_kernel,
        out_shape=(
            jax.ShapeDtypeStruct((CAP, F1), BF16),
            jax.ShapeDtypeStruct((CAP, F2), BF16),
            jax.ShapeDtypeStruct((EXPERTS, ROWS_DEV), F32),
        ),
        in_specs=[VMEM, VMEM],
        out_specs=(VMEM,) * 3,
        name="arrive",
    )(got, own_placing)

    first_z = across_z(first)
    second_left, second_right = along_y(second, 1), along_y(second, -1)
    second_z = across_z(second)
    pair = jnp.concatenate([first, first_z], axis=0)
    pair_left, pair_right = along_y(pair, 1), along_y(pair, -1)
    second_far_a = along_y(second_left[:, : F2 // 2], 1)
    second_far_b = along_y(second_right[:, F2 // 2 :], -1)
    second_left_z = across_z(second_left)
    second_right_z = across_z(second_right)
    pair_far_a = along_y(pair_left[:, : F1 // 2], 1)
    pair_far_b = along_y(pair_right[:, F1 // 2 :], -1)
    second_far_az = across_z(second_far_a)
    second_far_bz = across_z(second_far_b)

    weights = (gate_own, gate_other, up_own, up_other)
    partial = gate_call(
        gate_first,
        (pair, pair_left, pair_right, pair_far_a, pair_far_b),
        ((0, 0), (80, 0), (160, 0), (240, 0), (240, F1 // 2)),
        (),
        weights,
        0,
        F1,
        2,
        F32,
    )
    (hidden,) = gate_call(
        gate_last,
        (
            second,
            second_z,
            second_left,
            second_left_z,
            second_right,
            second_right_z,
            second_far_a,
            second_far_b,
            second_far_az,
            second_far_bz,
        ),
        (
            (0, 0),
            (40, 0),
            (80, 0),
            (120, 0),
            (160, 0),
            (200, 0),
            (240, 0),
            (240, F2 // 2),
            (280, 0),
            (280, F2 // 2),
        ),
        partial,
        weights,
        F1 // F2,
        F2,
        1,
        BF16,
    )

    part_two = down_call(hidden, down_own, down_other, F1, F2, 1024)
    part_one = down_call(hidden, down_own, down_other, 0, F1, 1024)
    two = part_two.reshape(N_Y, 2, CAP, F2)
    two_z = across_z(two[:, 1])
    one = [part_one[80 * i : 80 * i + 80] for i in range(N_Y)]
    one = add(*scatter_y(*one))
    two = add(two[:, 0], two_z)
    two = add(*scatter_y(two[0], two[1], two[2], two[3]))
    one = add(one[:CAP], across_z(one[CAP:]))
    result = jnp.concatenate([one, two], axis=1)
    result = result.reshape(CAP, EXPERTS, WIDTH).transpose(1, 0, 2)
    returned = lax.all_to_all(result, "exp", split_axis=0, concat_axis=0, tiled=True)

    onehot = expert_ids[:, :, None] == expert_range[None, None, :]
    chosen = jnp.sum(jnp.where(onehot, logits.T[:, None, :], 0.0), axis=-1)
    route_weight = jax.nn.sigmoid(chosen - chosen[:, ::-1])
    mix_shape = jax.ShapeDtypeStruct((ROWS_DEV, SLOTS), BF16)
    mix_hi, mix_lo = pl.pallas_call(
        mixing_kernel,
        out_shape=(mix_shape, mix_shape),
        in_specs=[VMEM, VMEM],
        out_specs=(VMEM, VMEM),
        name="mixing",
    )(slot, route_weight)
    return pl.pallas_call(
        final_kernel,
        out_shape=jax.ShapeDtypeStruct((ROWS_DEV, WIDTH), BF16),
        in_specs=[VMEM] * 4,
        out_specs=VMEM,
        name="final",
    )(mix_hi, mix_lo, returned.reshape(SLOTS, WIDTH), carried)


def solution(mesh):
    placed = (
        P("ctx", "exp"),
        P(None, "ctx", "exp"),
        P(None, "ctx", "exp"),
        P("ctx", "exp"),
        P(None, "ctx", None, "exp"),
        P(None, "ctx", "exp"),
        P("ctx"),
        P("ctx", "exp"),
        P("exp"),
        P("exp", None),
        P("ctx", None),
        P(),
        P("exp", None, "ctx"),
        P("exp", None, "ctx"),
        P("exp", "ctx", None),
    )
    return jax.shard_map(
        on_device, mesh=mesh, in_specs=placed, out_specs=P("ctx", "exp"), check_vma=False
    )
```

```python
import functools

import jax
import jax.numpy as jnp
from jax import lax
from jax.experimental import pallas as pl
from jax.experimental.pallas import tpu as pltpu
from jax.sharding import PartitionSpec as P

D = 6144
HD = 128
QPK = 6
EXPERTS = 8
TOPK = 2
CAP = 40
FF_DEV = 512
SPAN_DEV = 128
ROWS_DEV = 144
N_Y = 4
WIDTH = D // EXPERTS
SLOTS = CAP * EXPERTS
MSG = QPK * HD + 128
EXTRA = 8

F1 = 4096
F2 = D - F1

NEG = -1e30
EPS = 1e-05
LOG2E = 1.4426950408889634
SCALE2 = HD ** (-0.5) * LOG2E
BF16 = jnp.bfloat16
F32 = jnp.float32
MIB = 2**20
VMEM = pl.BlockSpec(memory_space=pltpu.VMEM)
SMEM = pl.BlockSpec(memory_space=pltpu.SMEM)


def ctx_index(y, z, core):
    return y * 4 + z * 2 + core


def moved(value, place):
    pairs = []
    for y in range(N_Y):
        for z in range(2):
            for core in range(2):
                pairs.append((ctx_index(y, z, core), ctx_index(*place(y, z, core))))
    return lax.ppermute(value, "ctx", pairs)


def along_y(value, steps):
    return moved(value, lambda y, z, core: ((y + steps) % N_Y, z, core))


def across_z(value):
    return moved(value, lambda y, z, core: (y, 1 - z, core))


def across_core(value):
    return moved(value, lambda y, z, core: (y, z, 1 - core))


def dot_nt(a, b, precision=None):
    return lax.dot_general(
        a, b, (((1,), (1,)), ((), ())), preferred_element_type=F32, precision=precision
    )


def split3(value):
    hi = value.astype(BF16).astype(F32)
    rest = value - hi
    mid = rest.astype(BF16).astype(F32)
    return hi, mid, rest - mid


def flash_kernel(place_ref, q_ref, b0, b1, b2, b3, msg_ref):
    blocks = (b0, b1, b2, b3)
    prompt = b0.shape[1] - SPAN_DEV
    rows = QPK * SPAN_DEV
    query = jnp.concatenate([q_ref[:, h * HD : (h + 1) * HD] for h in range(QPK)], axis=0)

    def scores_of(i):
        if i < len(blocks):
            return dot_nt(query, blocks[i][0, :prompt, :])
        keys = jnp.concatenate([block[0, prompt:, :] for block in blocks], axis=0)
        scores = dot_nt(query, keys)
        row = lax.broadcasted_iota(jnp.int32, scores.shape, 0) % SPAN_DEV
        col = lax.broadcasted_iota(jnp.int32, scores.shape, 1)
        block = col // SPAN_DEV
        source = jnp.where(
            block == 0,
            place_ref[1],
            jnp.where(block == 1, place_ref[2], jnp.where(block == 2, place_ref[3], place_ref[4])),
        )
        key = source * SPAN_DEV + col % SPAN_DEV
        return jnp.where(key <= row + place_ref[0] * SPAN_DEV, scores, NEG)

    def values_of(i):
        if i < len(blocks):
            values = blocks[i][1, :prompt, :]
        else:
            values = jnp.concatenate([block[1, prompt:, :] for block in blocks], axis=0)
        return jnp.concatenate([values, jnp.ones(values.shape, BF16)], axis=1)

    top = jnp.full((rows, 1), NEG, F32)
    summed = jnp.zeros((rows, 2 * HD), F32)
    scores = scores_of(0)
    for i in range(len(blocks) + 1):
        following = scores_of(i + 1) if i < len(blocks) else None
        newest = jnp.maximum(top, jnp.max(scores, axis=1, keepdims=True))
        probs = jnp.exp2((scores - newest) * SCALE2).astype(BF16)
        factor = jnp.exp2((top - newest) * SCALE2)
        summed = summed * factor + jnp.dot(probs, values_of(i), preferred_element_type=F32)
        top, scores = newest, following
    lane = lax.broadcasted_iota(jnp.int32, (SPAN_DEV, 128), 1)
    stats = jnp.zeros((SPAN_DEV, 128), F32)
    for h in range(QPK):
        at = slice(h * SPAN_DEV, (h + 1) * SPAN_DEV)
        total = summed[at, HD:]
        msg_ref[:, h * HD : (h + 1) * HD] = (summed[at, :HD] / total).astype(BF16)
        for i, part in enumerate(split3(top[at] * SCALE2 + jnp.log2(total))):
            stats = jnp.where(lane == 3 * h + i, part, stats)
    msg_ref[:, QPK * HD :] = stats.astype(BF16)


def flash_call(place, queries, blocks):
    return pl.pallas_call(
        flash_kernel,
        out_shape=jax.ShapeDtypeStruct((SPAN_DEV, MSG), BF16),
        in_specs=[SMEM] + [VMEM] * 5,
        out_specs=VMEM,
        compiler_params=pltpu.CompilerParams(vmem_limit_bytes=20 * MIB),
        cost_estimate=pl.CostEstimate(
            flops=8 * 768 * 4608 * 128, bytes_accessed=4 * MIB, transcendentals=768 * 4608
        ),
        name="flash",
    )(place, queries, *blocks)


def dispatch_kernel(
    m0, m1, m2, m3, decode_ref, residual_ref, gain_ref, router_ref, placing_ref, carried_ref, out_ref
):
    msgs = (m0, m1, m2, m3)
    for h in range(QPK):
        lanes = slice(h * HD, (h + 1) * HD)
        levels = []
        for m in msgs:
            at = QPK * HD + 3 * h
            stat = m[:, at : at + 3].astype(F32)
            levels.append(stat[:, 0:1] + stat[:, 1:2] + stat[:, 2:3])
        top = functools.reduce(jnp.maximum, levels)
        weights = [jnp.exp2(level - top) for level in levels]
        total = sum(weights)
        summed = sum(w * m[:, lanes].astype(F32) for w, m in zip(weights, msgs))
        attn = (summed / total).astype(BF16).astype(F32)
        carried_ref[:SPAN_DEV, lanes] = residual_ref[:SPAN_DEV, lanes].astype(F32) + attn
    carried_ref[SPAN_DEV:, :] = residual_ref[SPAN_DEV:, :].astype(F32) + decode_ref[...].astype(F32)
    carried = carried_ref[...]
    gained = carried * gain_ref[...].astype(F32)
    logits = dot_nt(router_ref[...].astype(F32), gained, lax.Precision.HIGHEST)
    squares = dot_nt(jnp.ones((EXTRA, WIDTH), F32), carried * carried, lax.Precision.HIGHEST)
    log_hi, log_mid, _ = split3(logits)
    sq_hi, sq_mid, _ = split3(squares)
    row = lax.broadcasted_iota(jnp.int32, squares.shape, 0)
    sq = jnp.where(row == 0, sq_hi, sq_mid)
    placed = jnp.dot(placing_ref[...], gained.astype(BF16), preferred_element_type=F32).astype(BF16)
    for e in range(EXPERTS):
        out_ref[e, :CAP, :] = placed[e * CAP : (e + 1) * CAP, :]
        out_ref[e, CAP:, :] = jnp.zeros((EXTRA, WIDTH), BF16)
        out_ref[e, CAP:, 0:ROWS_DEV] = log_hi.astype(BF16)
        out_ref[e, CAP:, 256 : 256 + ROWS_DEV] = log_mid.astype(BF16)
        out_ref[e, CAP:, 512 : 512 + ROWS_DEV] = sq.astype(BF16)


def arrive_kernel(got_ref, placing_ref, x_ref, first_ref, logits_ref):
    stats = got_ref[0, CAP:, :].astype(F32)
    for e in range(1, EXPERTS):
        stats = stats + got_ref[e, CAP:, :].astype(F32)
    logits = stats[:, 0:ROWS_DEV] + stats[:, 256 : 256 + ROWS_DEV]
    squares = stats[0:1, 512 : 512 + ROWS_DEV] + stats[1:2, 512 : 512 + ROWS_DEV]
    rscale = lax.rsqrt(squares / D + EPS)
    logits_ref[...] = logits * rscale
    scale = jnp.sum(placing_ref[...].astype(F32) * rscale, axis=1, keepdims=True)
    for e in range(EXPERTS):
        rows = (got_ref[e, :CAP, :].astype(F32) * scale).astype(BF16)
        begin = e * WIDTH
        end = begin + WIDTH
        x_ref[:, begin:end] = rows
        if begin < F1:
            first_ref[:, begin : min(end, F1)] = rows[:, : min(end, F1) - begin]


HALF = D // 2
HALF1 = F1 // 2
N_TILE = 256
DEPTH = D // 2
OUT_TILE = 1024
AHEAD = 6
N_SLOTS = 3
HBM = pl.BlockSpec(memory_space=pltpu.HBM)


def piece_places():
    places = [(0, 0, 0, 0), (1, 0, 0, 2), (2, 0, 0, 4)]
    places += [(3, 0, 0, 1), (4, 0, 0, 3), (5, 0, 0, 5)]
    places += [(6, 0, F1, 1), (6, CAP, F1, 3), (6, 2 * CAP, F1, 5)]
    places += [(7, 0, 0, 6), (8, 0, HALF, 6)]
    places += [(9, 0, 0, 7), (10, 0, HALF1, 7), (11, 0, F1, 7)]
    return places


N_PIECES = 12


def expert_kernel(*refs):
    pieces, weights = refs[:N_PIECES], refs[N_PIECES : N_PIECES + 6]
    outs, (x_ref, hidden_ref, gate_buf, down_buf, sems) = refs[N_PIECES + 6 : -5], refs[-5:]
    copies = []
    for i in range(2):
        for n in range(FF_DEV // N_TILE):
            for k in range(D // DEPTH):
                for w in range(2):
                    rows, cols = pl.ds(k * DEPTH, DEPTH), pl.ds(n * N_TILE, N_TILE)
                    slot = (i * 2 + n) % N_SLOTS * 2 + w
                    copies.append(
                        (weights[2 * w + i].at[0, rows, cols], gate_buf.at[slot, rows, :])
                    )
    for j in range(D // OUT_TILE):
        for i in range(2):
            cols = pl.ds(j * OUT_TILE, OUT_TILE)
            copies.append((weights[4 + i].at[0, :, cols], down_buf.at[i, :, cols]))
    copies = [pltpu.make_async_copy(src, dst, sems.at[i]) for i, (src, dst) in enumerate(copies)]
    for copy in copies[:AHEAD]:
        copy.start()
    done = 0

    def arrived():
        nonlocal done
        for _ in range(2):
            if done + AHEAD < len(copies):
                copies[done + AHEAD].start()
            copies[done].wait()
            done += 1

    for piece, top, col, block in piece_places():
        width = pieces[piece].shape[1]
        x_ref[block * CAP : (block + 1) * CAP, col : col + width] = pieces[piece][
            top : top + CAP, :
        ]
    for tile in range(2 * FF_DEV // N_TILE):
        gate = up = None
        for k in range(D // DEPTH):
            arrived()
            at = slice(k * DEPTH, (k + 1) * DEPTH)
            x = x_ref[:, at]
            gate_k = jnp.dot(x, gate_buf[tile % N_SLOTS * 2, at, :], preferred_element_type=F32)
            up_k = jnp.dot(x, gate_buf[tile % N_SLOTS * 2 + 1, at, :], preferred_element_type=F32)
            gate = gate_k if gate is None else gate + gate_k
            up = up_k if up is None else up + up_k
        hidden = gate / (1.0 + jnp.exp(-gate)) * up
        hidden_ref[:, tile * N_TILE : (tile + 1) * N_TILE] = hidden.astype(BF16)

    own, left, right, far_a, far_b, own_z, left_z, right_z, far_z_a, far_z_b, stack, far_two = outs
    for j in range(D // OUT_TILE):
        arrived()
        begin = j * OUT_TILE
        at = slice(begin, begin + OUT_TILE)
        out = jnp.dot(hidden_ref[:, :FF_DEV], down_buf[0, :, at], preferred_element_type=F32)
        out = out + jnp.dot(hidden_ref[:, FF_DEV:], down_buf[1, :, at], preferred_element_type=F32)
        terms = [out[i * CAP : (i + 1) * CAP].astype(BF16) for i in range(8)]
        own[:, at], left[:, at], right[:, at] = terms[0], terms[2], terms[4]
        if begin < HALF:
            far_a[:, at] = terms[6]
        else:
            far_b[:, begin - HALF : begin - HALF + OUT_TILE] = terms[6]
        if begin < F1:
            own_z[:, at], left_z[:, at], right_z[:, at] = terms[1], terms[3], terms[5]
            if begin < HALF1:
                far_z_a[:, at] = terms[7]
            else:
                far_z_b[:, begin - HALF1 : begin - HALF1 + OUT_TILE] = terms[7]
        else:
            at = slice(begin - F1, begin - F1 + OUT_TILE)
            far_two[:, at] = terms[7]
            for i in range(3):
                stack[i * CAP : (i + 1) * CAP, at] = terms[2 * i + 1]


def rows_of(rows, width):
    return jax.ShapeDtypeStruct((rows, width), BF16)


def expert_call(pieces, weights):
    outs = (rows_of(CAP, D),) * 3 + (rows_of(CAP, HALF),) * 2
    outs += (rows_of(CAP, F1),) * 3 + (rows_of(CAP, HALF1),) * 2
    outs += (rows_of(3 * CAP, F2), rows_of(CAP, F2))
    n_copies = 2 * (FF_DEV // N_TILE) * (D // DEPTH) * 2 + 2 * (D // OUT_TILE)
    return pl.pallas_call(
        expert_kernel,
        out_shape=outs,
        in_specs=[VMEM] * N_PIECES + [HBM] * 6,
        out_specs=(VMEM,) * len(outs),
        scratch_shapes=[
            pltpu.VMEM((SLOTS, D), BF16),
            pltpu.VMEM((SLOTS, 2 * FF_DEV), BF16),
            pltpu.VMEM((2 * N_SLOTS, D, N_TILE), BF16),
            pltpu.VMEM((2, FF_DEV, D), BF16),
            pltpu.SemaphoreType.DMA((n_copies,)),
        ],
        compiler_params=pltpu.CompilerParams(vmem_limit_bytes=42 * MIB),
        cost_estimate=pl.CostEstimate(
            flops=2 * SLOTS * D * 6 * FF_DEV, bytes_accessed=44 * MIB, transcendentals=0
        ),
        name="experts",
    )(*pieces, *weights)


def add(*values):
    return functools.reduce(jnp.add, [v.astype(F32) for v in values]).astype(BF16)


def widen(value, begin, width):
    return jnp.pad(value, ((0, 0), (begin, width - begin - value.shape[1])))


def final_kernel(hi_ref, lo_ref, got_ref, carried_ref, out_ref):
    got = got_ref[...]
    moe = jnp.dot(hi_ref[...], got, preferred_element_type=F32)
    moe = moe + jnp.dot(lo_ref[...], got, preferred_element_type=F32)
    out_ref[...] = (carried_ref[...] + moe).astype(BF16)


def mixing_kernel(slot_ref, weight_ref, hi_ref, lo_ref):
    lane = lax.broadcasted_iota(jnp.int32, (ROWS_DEV, SLOTS), 1)
    mix = jnp.zeros((ROWS_DEV, SLOTS), F32)
    for k in range(TOPK):
        mix = jnp.where(slot_ref[:, k : k + 1] == lane, weight_ref[:, k : k + 1], mix)
    hi = mix.astype(BF16)
    hi_ref[...] = hi
    lo_ref[...] = (mix - hi.astype(F32)).astype(BF16)


def decode_block(decode_q, decode_cache, decode_new, decode_len):
    rows = decode_q.shape[0]
    length = decode_cache.shape[2]
    queries = decode_q.reshape(rows, QPK, HD)
    keys = decode_cache[0]
    values = decode_cache[1]
    own_key = decode_new[0]
    own_value = decode_new[1]
    scale = HD ** (-0.5)
    scores = jnp.einsum("rqd,rld->rql", queries, keys, preferred_element_type=F32) * scale
    live = (jnp.arange(length, dtype=jnp.int32)[None, :] < decode_len[:, None])[:, None, :]
    own = jnp.einsum("rqd,rd->rq", queries, own_key, preferred_element_type=F32) * scale
    top = jnp.maximum(jnp.max(jnp.where(live, scores, NEG), axis=-1), own)
    weights = jnp.where(live, jnp.exp(scores - top[..., None]), 0.0)
    own_weight = jnp.exp(own - top)
    own_prob = lax.optimization_barrier(own_weight.astype(BF16)).astype(F32)
    summed = jnp.einsum("rql,rld->rqd", weights.astype(BF16), values, preferred_element_type=F32)
    summed = summed + own_prob[..., None] * own_value.astype(F32)[:, None, :]
    result = summed / (jnp.sum(weights, axis=-1) + own_weight)[..., None]
    return result.reshape(rows, QPK * HD).astype(BF16)


def on_device(
    span_q,
    prompt_kv,
    span_kv,
    decode_q,
    decode_cache,
    decode_new,
    decode_len,
    residual,
    norm_gain,
    router,
    expert_ids,
    capacity,
    w_gate,
    w_up,
    w_down,
):
    here = lax.axis_index("ctx")
    y, z, core = here // 4, (here // 2) % 2, here % 2
    kv = jnp.concatenate([prompt_kv, span_kv], axis=1)
    kv_z = across_z(kv)
    kv_core = across_core(kv)
    q_left, q_right, q_far = along_y(span_q, 1), along_y(span_q, -1), along_y(span_q, 2)
    kv_zc = across_core(kv_z)
    expert_range = jnp.arange(EXPERTS, dtype=jnp.int32)
    flat_ids = expert_ids.reshape(ROWS_DEV * TOPK)
    assign = (flat_ids[:, None] == expert_range[None, :]).astype(jnp.int32)
    prior = jnp.cumsum(assign, axis=0) - assign
    position = jnp.sum(prior * assign, axis=1)
    limit = jnp.sum(assign * capacity[None, :], axis=1)
    slot = jnp.where(position < limit, flat_ids * CAP + position, -1).reshape(ROWS_DEV, TOPK)
    slot_range = jnp.arange(SLOTS, dtype=jnp.int32)[:, None]
    placing = ((slot[:, 0][None, :] == slot_range) | (slot[:, 1][None, :] == slot_range)).astype(
        BF16
    )
    own_placing = lax.dynamic_slice_in_dim(placing, lax.axis_index("exp") * CAP, CAP, 0)

    decode_out = decode_block(decode_q, decode_cache, decode_new, decode_len)
    gate_own, gate_other = w_gate, across_core(w_gate)
    kv_core, kv_z, kv_zc, q_left, q_right, gate_other, decode_out, placing, slot = (
        lax.optimization_barrier(
            (kv_core, kv_z, kv_zc, q_left, q_right, gate_other, decode_out, placing, slot)
        )
    )
    blocks = (kv, kv_core, kv_z, kv_zc)
    sources = [
        ctx_index(y, a, b) for a, b in ((z, core), (z, 1 - core), (1 - z, core), (1 - z, 1 - core))
    ]

    def attend(steps, queries):
        place = jnp.stack([ctx_index((y + steps) % N_Y, z, core)] + sources).astype(jnp.int32)
        return flash_call(place, queries, blocks)

    up_own, down_own, q_left = lax.optimization_barrier((w_up, w_down, q_left))
    up_other, down_other = across_core(up_own), across_core(down_own)
    part = attend(-1, q_left)
    msg_right = along_y(part, -1)
    q_right, q_far, part = lax.optimization_barrier((q_right, q_far, part))
    msg_left = along_y(attend(1, q_right), 1)
    msg_far = along_y(attend(2, q_far), 2)
    msg_own = attend(0, span_q)
    msg_far, msg_left, msg_right, msg_own, up_other, down_other = lax.optimization_barrier(
        (msg_far, msg_left, msg_right, msg_own, up_other, down_other)
    )

    carried, outgoing = pl.pallas_call(
        dispatch_kernel,
        out_shape=(
            jax.ShapeDtypeStruct((ROWS_DEV, WIDTH), F32),
            jax.ShapeDtypeStruct((EXPERTS, CAP + EXTRA, WIDTH), BF16),
        ),
        in_specs=[VMEM] * 9,
        out_specs=(VMEM, VMEM),
        name="dispatch",
    )(
        msg_own,
        msg_far,
        msg_left,
        msg_right,
        decode_out,
        residual,
        norm_gain.reshape(1, WIDTH),
        router.T,
        placing,
    )
    got = lax.all_to_all(outgoing, "exp", split_axis=0, concat_axis=0, tiled=True)
    x, first, logits = pl.pallas_call(
        arrive_kernel,
        out_shape=(
            jax.ShapeDtypeStruct((CAP, D), BF16),
            jax.ShapeDtypeStruct((CAP, F1), BF16),
            jax.ShapeDtypeStruct((EXPERTS, ROWS_DEV), F32),
        ),
        in_specs=[VMEM, VMEM],
        out_specs=(VMEM,) * 3,
        name="arrive",
    )(got, own_placing)

    first_z = across_z(first)
    x_left, x_right = along_y(x, 1), along_y(x, -1)
    first_z, x_left, x_right = lax.optimization_barrier((first_z, x_left, x_right))
    far_a, far_b = along_y(x_left[:, :HALF], 1), along_y(x_right[:, HALF:], -1)
    first_z_left, first_z_right = along_y(first_z, 1), along_y(first_z, -1)
    stack_z = across_z(jnp.concatenate([x[:, F1:], x_left[:, F1:], x_right[:, F1:]], axis=0))
    stack_z, first_z_left, first_z_right, far_a, far_b = lax.optimization_barrier(
        (stack_z, first_z_left, first_z_right, far_a, far_b)
    )
    far_z_a = along_y(first_z_left[:, :HALF1], 1)
    far_z_b = along_y(first_z_right[:, HALF1:], -1)
    far_z_two = across_z(far_b[:, F1 - HALF :])
    pieces = (x, x_left, x_right, first_z, first_z_left, first_z_right, stack_z)
    pieces += (far_a, far_b, far_z_a, far_z_b, far_z_two)
    terms = expert_call(pieces, (gate_own, gate_other, up_own, up_other, down_own, down_other))

    own, left, right, far_a, far_b, own_z, left_z, right_z, far_z_a, far_z_b, stack, far_two = terms
    got_two = across_z(far_two)
    got_left, got_right = along_y(far_z_a, 1), along_y(far_z_b, -1)
    stack = across_z(stack)
    right_z = add(right_z, widen(got_left, 0, F1))
    left_z = add(left_z, widen(got_right, HALF1, F1))
    far_b = add(far_b, widen(got_two, F1 - HALF, HALF))
    z_left, z_right = along_y(right_z, 1), along_y(left_z, -1)
    got_a, got_b = along_y(far_a, 1), along_y(far_b, -1)
    z_left, z_right, got_a, got_b, stack = lax.optimization_barrier(
        (z_left, z_right, got_a, got_b, stack)
    )
    own_z = add(own_z, z_left, z_right)
    right = add(right, widen(got_a, 0, D), widen(stack[2 * CAP :], F1, D))
    left = add(left, widen(got_b, HALF, D), widen(stack[CAP : 2 * CAP], F1, D))
    got_left, got_right = along_y(right, 1), along_y(left, -1)
    got_z = across_z(own_z)
    result = add(own, got_left, got_right, widen(got_z, 0, D), widen(stack[:CAP], F1, D))
    result = result.reshape(CAP, EXPERTS, WIDTH).transpose(1, 0, 2)
    returned = lax.all_to_all(result, "exp", split_axis=0, concat_axis=0, tiled=True)

    onehot = expert_ids[:, :, None] == expert_range[None, None, :]
    chosen = jnp.sum(jnp.where(onehot, logits.T[:, None, :], 0.0), axis=-1)
    route_weight = jax.nn.sigmoid(chosen - chosen[:, ::-1])
    mix_shape = jax.ShapeDtypeStruct((ROWS_DEV, SLOTS), BF16)
    mix_hi, mix_lo = pl.pallas_call(
        mixing_kernel,
        out_shape=(mix_shape, mix_shape),
        in_specs=[VMEM, VMEM],
        out_specs=(VMEM, VMEM),
        name="mixing",
    )(slot, route_weight)
    return pl.pallas_call(
        final_kernel,
        out_shape=jax.ShapeDtypeStruct((ROWS_DEV, WIDTH), BF16),
        in_specs=[VMEM] * 4,
        out_specs=VMEM,
        name="final",
    )(mix_hi, mix_lo, returned.reshape(SLOTS, WIDTH), carried)


def solution(mesh):
    placed = (
        P("ctx", "exp"),
        P(None, "ctx", "exp"),
        P(None, "ctx", "exp"),
        P("ctx", "exp"),
        P(None, "ctx", None, "exp"),
        P(None, "ctx", "exp"),
        P("ctx"),
        P("ctx", "exp"),
        P("exp"),
        P("exp", None),
        P("ctx", None),
        P(),
        P("exp", None, "ctx"),
        P("exp", None, "ctx"),
        P("exp", "ctx", None),
    )
    return jax.shard_map(
        on_device, mesh=mesh, in_specs=placed, out_specs=P("ctx", "exp"), check_vma=False
    )
```

```python
import functools

import jax
import jax.numpy as jnp
from jax import lax
from jax.experimental import pallas as pl
from jax.experimental.pallas import tpu as pltpu
from jax.sharding import PartitionSpec as P

D = 6144
HD = 128
QPK = 6
EXPERTS = 8
TOPK = 2
CAP = 40
FF_DEV = 512
SPAN_DEV = 128
ROWS_DEV = 144
N_Y = 4
WIDTH = D // EXPERTS
SLOTS = CAP * EXPERTS
MSG = QPK * HD + 128
EXTRA = 8

F1 = 4096
F2 = D - F1

NEG = -1e30
EPS = 1e-05
LOG2E = 1.4426950408889634
SCALE2 = HD ** (-0.5) * LOG2E
BF16 = jnp.bfloat16
F32 = jnp.float32
MIB = 2**20
VMEM = pl.BlockSpec(memory_space=pltpu.VMEM)
SMEM = pl.BlockSpec(memory_space=pltpu.SMEM)


def ctx_index(y, z, core):
    return y * 4 + z * 2 + core


def moved(value, place):
    pairs = []
    for y in range(N_Y):
        for z in range(2):
            for core in range(2):
                pairs.append((ctx_index(y, z, core), ctx_index(*place(y, z, core))))
    return lax.ppermute(value, "ctx", pairs)


def along_y(value, steps):
    return moved(value, lambda y, z, core: ((y + steps) % N_Y, z, core))


def across_z(value):
    return moved(value, lambda y, z, core: (y, 1 - z, core))


def across_core(value):
    return moved(value, lambda y, z, core: (y, z, 1 - core))


def dot_nt(a, b, precision=None):
    return lax.dot_general(
        a, b, (((1,), (1,)), ((), ())), preferred_element_type=F32, precision=precision
    )


def split3(value):
    hi = value.astype(BF16).astype(F32)
    rest = value - hi
    mid = rest.astype(BF16).astype(F32)
    return hi, mid, rest - mid


def flash_steps(place_ref, first, q_ref, blocks, state):
    prompt = blocks[0].shape[1] - SPAN_DEV
    query = jnp.concatenate([q_ref[:, h * HD : (h + 1) * HD] for h in range(QPK)], axis=0)

    def scores_of(i):
        if i < len(blocks):
            return dot_nt(query, blocks[i][0, :prompt, :])
        keys = jnp.concatenate([block[0, prompt:, :] for block in blocks], axis=0)
        scores = dot_nt(query, keys)
        row = lax.broadcasted_iota(jnp.int32, scores.shape, 0) % SPAN_DEV
        col = lax.broadcasted_iota(jnp.int32, scores.shape, 1)
        block = col // SPAN_DEV
        source = jnp.full(scores.shape, place_ref[first], jnp.int32)
        for j in range(1, len(blocks)):
            source = jnp.where(block == j, place_ref[first + j], source)
        key = source * SPAN_DEV + col % SPAN_DEV
        return jnp.where(key <= row + place_ref[0] * SPAN_DEV, scores, NEG)

    def values_of(i):
        if i < len(blocks):
            values = blocks[i][1, :prompt, :]
        else:
            values = jnp.concatenate([block[1, prompt:, :] for block in blocks], axis=0)
        return jnp.concatenate([values, jnp.ones(values.shape, BF16)], axis=1)

    top, summed = state
    scores = scores_of(0)
    for i in range(len(blocks) + 1):
        following = scores_of(i + 1) if i < len(blocks) else None
        newest = jnp.max(scores, axis=1, keepdims=True)
        if top is not None:
            newest = jnp.maximum(top, newest)
        probs = jnp.exp2((scores - newest) * SCALE2).astype(BF16)
        part = jnp.dot(probs, values_of(i), preferred_element_type=F32)
        summed = part if top is None else summed * jnp.exp2((top - newest) * SCALE2) + part
        top, scores = newest, following
    return top, summed


def write_message(top, summed, msg_ref):
    lane = lax.broadcasted_iota(jnp.int32, (SPAN_DEV, 128), 1)
    stats = jnp.zeros((SPAN_DEV, 128), F32)
    for h in range(QPK):
        at = slice(h * SPAN_DEV, (h + 1) * SPAN_DEV)
        total = summed[at, HD:]
        msg_ref[:, h * HD : (h + 1) * HD] = (summed[at, :HD] / total).astype(BF16)
        for i, part in enumerate(split3(top[at] * SCALE2 + jnp.log2(total))):
            stats = jnp.where(lane == 3 * h + i, part, stats)
    msg_ref[:, QPK * HD :] = stats.astype(BF16)


def flash_all(place_ref, q_ref, b0, b1, b2, b3, msg_ref):
    top, summed = flash_steps(place_ref, 1, q_ref, (b0, b1, b2, b3), (None, None))
    write_message(top, summed, msg_ref)


def flash_call(place, queries, blocks):
    rows = QPK * SPAN_DEV
    count = len(blocks) * blocks[0].shape[1]
    return pl.pallas_call(
        flash_all,
        out_shape=jax.ShapeDtypeStruct((SPAN_DEV, MSG), BF16),
        in_specs=[SMEM] + [VMEM] * (1 + len(blocks)),
        out_specs=VMEM,
        compiler_params=pltpu.CompilerParams(vmem_limit_bytes=20 * MIB),
        cost_estimate=pl.CostEstimate(
            flops=8 * rows * count * HD, bytes_accessed=4 * MIB, transcendentals=rows * count
        ),
        name="flash",
    )(place, queries, *blocks)


def dispatch_kernel(
    m0, m1, m2, m3, decode_ref, residual_ref, gain_ref, router_ref, placing_ref, carried_ref, out_ref
):
    msgs = (m0, m1, m2, m3)
    for h in range(QPK):
        lanes = slice(h * HD, (h + 1) * HD)
        levels = []
        for m in msgs:
            at = QPK * HD + 3 * h
            stat = m[:, at : at + 3].astype(F32)
            levels.append(stat[:, 0:1] + stat[:, 1:2] + stat[:, 2:3])
        top = functools.reduce(jnp.maximum, levels)
        weights = [jnp.exp2(level - top) for level in levels]
        total = sum(weights)
        summed = sum(w * m[:, lanes].astype(F32) for w, m in zip(weights, msgs))
        attn = (summed / total).astype(BF16).astype(F32)
        carried_ref[:SPAN_DEV, lanes] = residual_ref[:SPAN_DEV, lanes].astype(F32) + attn
    carried_ref[SPAN_DEV:, :] = residual_ref[SPAN_DEV:, :].astype(F32) + decode_ref[...].astype(F32)
    carried = carried_ref[...]
    gained = carried * gain_ref[...].astype(F32)
    logits = sum(dot_nt(router_ref[...], part.astype(BF16)) for part in split3(gained))
    ones = jnp.ones((EXTRA, WIDTH), BF16)
    squares = sum(dot_nt(ones, part.astype(BF16)) for part in split3(carried * carried))
    log_hi, log_mid, _ = split3(logits)
    sq_hi, sq_mid, _ = split3(squares)
    row = lax.broadcasted_iota(jnp.int32, squares.shape, 0)
    sq = jnp.where(row == 0, sq_hi, sq_mid)
    placed = jnp.dot(placing_ref[...], gained.astype(BF16), preferred_element_type=F32).astype(BF16)
    for e in range(EXPERTS):
        out_ref[e, :CAP, :] = placed[e * CAP : (e + 1) * CAP, :]
        out_ref[e, CAP:, :] = jnp.zeros((EXTRA, WIDTH), BF16)
        out_ref[e, CAP:, 0:ROWS_DEV] = log_hi.astype(BF16)
        out_ref[e, CAP:, 256 : 256 + ROWS_DEV] = log_mid.astype(BF16)
        out_ref[e, CAP:, 512 : 512 + ROWS_DEV] = sq.astype(BF16)


def arrive_kernel(expert_ref, got_ref, placing_ref, x_ref, first_ref, logits_ref):
    stats = got_ref[0, CAP:, :].astype(F32)
    for e in range(1, EXPERTS):
        stats = stats + got_ref[e, CAP:, :].astype(F32)
    logits = stats[:, 0:ROWS_DEV] + stats[:, 256 : 256 + ROWS_DEV]
    squares = stats[0:1, 512 : 512 + ROWS_DEV] + stats[1:2, 512 : 512 + ROWS_DEV]
    rscale = lax.rsqrt(squares / D + EPS)
    logits_ref[...] = logits * rscale
    placing = placing_ref[pl.ds(pl.multiple_of(expert_ref[0] * CAP, 8), CAP), :]
    scale = jnp.sum(placing * rscale, axis=1, keepdims=True)
    for e in range(EXPERTS):
        rows = (got_ref[e, :CAP, :].astype(F32) * scale).astype(BF16)
        begin = e * WIDTH
        end = begin + WIDTH
        x_ref[:, begin:end] = rows
        if begin < F1:
            first_ref[:, begin : min(end, F1)] = rows[:, : min(end, F1) - begin]


HALF = D // 2
HALF1 = F1 // 2
N_TILE = 256
DEPTH = D // 2
OUT_TILE = 1024
AHEAD = 6
N_SLOTS = 3
HBM = pl.BlockSpec(memory_space=pltpu.HBM)


def piece_places():
    places = [(0, 0, 0, D, 0, 0), (1, 0, 0, D, 0, 2), (2, 0, 0, D, 0, 4)]
    places += [(3, 0, 0, F1, 0, 1), (4, 0, 0, F1, 0, 3), (5, 0, 0, F1, 0, 5)]
    places += [(6, i * CAP, 0, F2, F1, 2 * i + 1) for i in range(3)]
    places += [(7, 0, 0, HALF, 0, 6), (8, 0, 0, HALF, HALF, 6)]
    places += [(9, 0, 0, HALF, 0, 7), (10, 0, 0, HALF, HALF, 7)]
    return places


N_PIECES = 11


def expert_kernel(*refs):
    pieces, weights = refs[:N_PIECES], refs[N_PIECES : N_PIECES + 6]
    outs, (x_ref, hidden_ref, gate_buf, down_buf, sems) = refs[N_PIECES + 6 : -5], refs[-5:]
    copies = []
    for i in range(2):
        for n in range(FF_DEV // N_TILE):
            for k in range(D // DEPTH):
                for w in range(2):
                    rows, cols = pl.ds(k * DEPTH, DEPTH), pl.ds(n * N_TILE, N_TILE)
                    slot = (i * 2 + n) % N_SLOTS * 2 + w
                    copies.append(
                        (weights[2 * w + i].at[0, rows, cols], gate_buf.at[slot, rows, :])
                    )
    for j in range(D // OUT_TILE):
        for i in range(2):
            cols = pl.ds(j * OUT_TILE, OUT_TILE)
            copies.append((weights[4 + i].at[0, :, cols], down_buf.at[i, :, cols]))
    copies = [pltpu.make_async_copy(src, dst, sems.at[i]) for i, (src, dst) in enumerate(copies)]
    for copy in copies[:AHEAD]:
        copy.start()
    done = 0

    def arrived():
        nonlocal done
        for _ in range(2):
            if done + AHEAD < len(copies):
                copies[done + AHEAD].start()
            copies[done].wait()
            done += 1

    for piece, top, begin, end, col, block in piece_places():
        x_ref[block * CAP : (block + 1) * CAP, col : col + end - begin] = pieces[piece][
            top : top + CAP, begin:end
        ]
    for tile in range(2 * FF_DEV // N_TILE):
        gate = up = None
        for k in range(D // DEPTH):
            arrived()
            at = slice(k * DEPTH, (k + 1) * DEPTH)
            x = x_ref[:, at]
            gate_k = jnp.dot(x, gate_buf[tile % N_SLOTS * 2, at, :], preferred_element_type=F32)
            up_k = jnp.dot(x, gate_buf[tile % N_SLOTS * 2 + 1, at, :], preferred_element_type=F32)
            gate = gate_k if gate is None else gate + gate_k
            up = up_k if up is None else up + up_k
        hidden = gate / (1.0 + jnp.exp(-gate)) * up
        hidden_ref[:, tile * N_TILE : (tile + 1) * N_TILE] = hidden.astype(BF16)

    own, left, right, far_a, far_b, own_z, left_z, right_z, far_z_a, far_z_b, stack, far_two = outs
    for j in range(D // OUT_TILE):
        arrived()
        begin = j * OUT_TILE
        at = slice(begin, begin + OUT_TILE)
        out = jnp.dot(hidden_ref[:, :FF_DEV], down_buf[0, :, at], preferred_element_type=F32)
        out = out + jnp.dot(hidden_ref[:, FF_DEV:], down_buf[1, :, at], preferred_element_type=F32)
        terms = [out[i * CAP : (i + 1) * CAP].astype(BF16) for i in range(8)]
        own[:, at], left[:, at], right[:, at] = terms[0], terms[2], terms[4]
        if begin < HALF:
            far_a[:, at] = terms[6]
        else:
            far_b[:, begin - HALF : begin - HALF + OUT_TILE] = terms[6]
        if begin < F1:
            own_z[:, at], left_z[:, at], right_z[:, at] = terms[1], terms[3], terms[5]
            if begin < HALF1:
                far_z_a[:, at] = terms[7]
            else:
                far_z_b[:, begin - HALF1 : begin - HALF1 + OUT_TILE] = terms[7]
        else:
            at = slice(begin - F1, begin - F1 + OUT_TILE)
            far_two[:, at] = terms[7]
            for i in range(3):
                stack[i * CAP : (i + 1) * CAP, at] = terms[2 * i + 1]


def rows_of(rows, width):
    return jax.ShapeDtypeStruct((rows, width), BF16)


def expert_call(pieces, weights):
    outs = (rows_of(CAP, D),) * 3 + (rows_of(CAP, HALF),) * 2
    outs += (rows_of(CAP, F1),) * 3 + (rows_of(CAP, HALF1),) * 2
    outs += (rows_of(3 * CAP, F2), rows_of(CAP, F2))
    n_copies = 2 * (FF_DEV // N_TILE) * (D // DEPTH) * 2 + 2 * (D // OUT_TILE)
    return pl.pallas_call(
        expert_kernel,
        out_shape=outs,
        in_specs=[VMEM] * N_PIECES + [HBM] * 6,
        out_specs=(VMEM,) * len(outs),
        scratch_shapes=[
            pltpu.VMEM((SLOTS, D), BF16),
            pltpu.VMEM((SLOTS, 2 * FF_DEV), BF16),
            pltpu.VMEM((2 * N_SLOTS, D, N_TILE), BF16),
            pltpu.VMEM((2, FF_DEV, D), BF16),
            pltpu.SemaphoreType.DMA((n_copies,)),
        ],
        compiler_params=pltpu.CompilerParams(vmem_limit_bytes=42 * MIB),
        cost_estimate=pl.CostEstimate(
            flops=2 * SLOTS * D * 6 * FF_DEV, bytes_accessed=44 * MIB, transcendentals=0
        ),
        name="experts",
    )(*pieces, *weights)


def add(*values):
    return functools.reduce(jnp.add, [v.astype(F32) for v in values]).astype(BF16)


def widen(value, begin, width):
    return jnp.pad(value, ((0, 0), (begin, width - begin - value.shape[1])))


def final_kernel(hi_ref, lo_ref, got_ref, carried_ref, out_ref):
    got = got_ref[...]
    moe = jnp.dot(hi_ref[...], got, preferred_element_type=F32)
    moe = moe + jnp.dot(lo_ref[...], got, preferred_element_type=F32)
    out_ref[...] = (carried_ref[...] + moe).astype(BF16)


def mixing_kernel(slot_ref, weight_ref, hi_ref, lo_ref):
    lane = lax.broadcasted_iota(jnp.int32, (ROWS_DEV, SLOTS), 1)
    mix = jnp.zeros((ROWS_DEV, SLOTS), F32)
    for k in range(TOPK):
        mix = jnp.where(slot_ref[:, k : k + 1] == lane, weight_ref[:, k : k + 1], mix)
    hi = mix.astype(BF16)
    hi_ref[...] = hi
    lo_ref[...] = (mix - hi.astype(F32)).astype(BF16)


def decode_kernel(len_ref, q_ref, cache_ref, new_ref, out_ref):
    count, length = cache_ref.shape[1], cache_ref.shape[2]
    rows = QPK * count
    query = jnp.concatenate([q_ref[:, h * HD : (h + 1) * HD] for h in range(QPK)], axis=0)
    row = lax.broadcasted_iota(jnp.int32, (rows, 1), 0) % count
    scores = jnp.zeros((rows, length), F32)
    lengths = jnp.zeros((rows, 1), jnp.int32)
    for r in range(count):
        scores = jnp.where(row == r, dot_nt(query, cache_ref[0, r]), scores)
        lengths = jnp.where(row == r, len_ref[r], lengths)
    key = jnp.concatenate([new_ref[0].astype(F32)] * QPK, axis=0)
    value = jnp.concatenate([new_ref[1].astype(F32)] * QPK, axis=0)
    own = jnp.sum(query.astype(F32) * key, axis=1, keepdims=True)
    live = lax.broadcasted_iota(jnp.int32, (rows, length), 1) < lengths
    top = jnp.maximum(jnp.max(jnp.where(live, scores, NEG), axis=1, keepdims=True), own)
    weights = jnp.where(live, jnp.exp2((scores - top) * SCALE2), 0.0)
    own_weight = jnp.exp2((own - top) * SCALE2)
    total = jnp.sum(weights, axis=1, keepdims=True) + own_weight
    summed = own_weight.astype(BF16).astype(F32) * value
    for r in range(count):
        probs = jnp.where(row == r, weights, 0.0).astype(BF16)
        summed = summed + jnp.dot(probs, cache_ref[1, r], preferred_element_type=F32)
    result = (summed / total).astype(BF16)
    for h in range(QPK):
        out_ref[:, h * HD : (h + 1) * HD] = result[h * count : (h + 1) * count]


def slots_kernel(capacity_ref, ids_ref, slot_ref, placing_ref, placing32_ref):
    lane = lax.broadcasted_iota(jnp.int32, (ROWS_DEV, 128), 1)
    ids = [ids_ref[:, k : k + 1] for k in range(TOPK)]
    named = [(lane == i).astype(F32) for i in ids]
    square = (ROWS_DEV, ROWS_DEV)
    earlier = lax.broadcasted_iota(jnp.int32, square, 0) > lax.broadcasted_iota(jnp.int32, square, 1)
    prior = jnp.dot(
        earlier.astype(F32).astype(BF16),
        (named[0] + named[1]).astype(BF16),
        preferred_element_type=F32,
    )
    limits = jnp.zeros((ROWS_DEV, 128), F32)
    for e in range(EXPERTS):
        limits = jnp.where(lane == e, capacity_ref[e].astype(F32), limits)
    wide = lax.broadcasted_iota(jnp.int32, (ROWS_DEV, 384), 1)
    placing = jnp.zeros((ROWS_DEV, 384), F32)
    for k in range(TOPK):
        position = jnp.sum(prior * named[k], axis=1, keepdims=True)
        limit = jnp.sum(limits * named[k], axis=1, keepdims=True)
        prior = prior + named[k]
        slot = jnp.where(position < limit, ids[k] * CAP + position.astype(jnp.int32), -1)
        slot_ref[:, k : k + 1] = slot
        placing = jnp.where(wide == slot, 1.0, placing)
    shape = (SLOTS, 384)
    same = lax.broadcasted_iota(jnp.int32, shape, 0) == lax.broadcasted_iota(jnp.int32, shape, 1)
    turned = dot_nt(same.astype(F32).astype(BF16), placing.astype(BF16))
    placing_ref[...] = turned.astype(BF16)
    placing32_ref[...] = turned


def on_device(
    span_q,
    prompt_kv,
    span_kv,
    decode_q,
    decode_cache,
    decode_new,
    decode_len,
    residual,
    norm_gain,
    router,
    expert_ids,
    capacity,
    w_gate,
    w_up,
    w_down,
):
    here = lax.axis_index("ctx")
    y, z, core = here // 4, (here // 2) % 2, here % 2
    kv = jnp.concatenate([prompt_kv, span_kv], axis=1)
    kv_z = across_z(kv)
    kv_core = across_core(kv)
    q_left, q_right = along_y(span_q, 1), along_y(span_q, -1)
    gate_own, gate_other = w_gate, across_core(w_gate)
    sources = [
        ctx_index(y, a, b) for a, b in ((z, core), (z, 1 - core), (1 - z, core), (1 - z, 1 - core))
    ]
    places = [
        jnp.stack([ctx_index((y + steps) % N_Y, z, core)] + sources).astype(jnp.int32)
        for steps in (-1, 1, 2, 0)
    ]
    decode_out = pl.pallas_call(
        decode_kernel,
        out_shape=jax.ShapeDtypeStruct(decode_q.shape, BF16),
        in_specs=[SMEM] + [VMEM] * 3,
        out_specs=VMEM,
        name="decode",
    )(decode_len, decode_q, decode_cache, decode_new)
    slot, placing, placing32 = pl.pallas_call(
        slots_kernel,
        out_shape=(
            jax.ShapeDtypeStruct((ROWS_DEV, TOPK), jnp.int32),
            jax.ShapeDtypeStruct((SLOTS, ROWS_DEV), BF16),
            jax.ShapeDtypeStruct((SLOTS, ROWS_DEV), F32),
        ),
        in_specs=[SMEM, VMEM],
        out_specs=(VMEM,) * 3,
        name="slots",
    )(capacity, expert_ids)
    gain = norm_gain.reshape(1, WIDTH)
    router_t = router.T
    q_left, decode_out, slot = lax.optimization_barrier((q_left, decode_out, slot))
    q_far = along_y(q_left, 1)
    waited = (kv_core, kv_z, q_left, q_right, q_far, gate_other, decode_out, gain, router_t)
    waited, places, weights, slots = lax.optimization_barrier(
        (waited, places, (w_up, w_down), (slot, placing, placing32))
    )
    kv_core, kv_z, q_left, q_right, q_far, gate_other, decode_out, gain, router_t = waited
    slot, placing, placing32 = slots
    kv_zc = across_core(kv_z)
    kv_zc, weights = lax.optimization_barrier((kv_zc, weights))
    up_own, down_own = weights
    up_other, down_other = [across_core(w) for w in weights]
    blocks = (kv, kv_core, kv_z, kv_zc)
    part_far = flash_call(places[2], q_far, blocks)
    msg_far = along_y(part_far, 2)
    part_left = flash_call(places[0], q_left, blocks)
    msg_right = along_y(part_left, -1)
    q_right, part_far, part_left = lax.optimization_barrier((q_right, part_far, part_left))
    msg_left = along_y(flash_call(places[1], q_right, blocks), 1)
    msg_own = flash_call(places[3], span_q, blocks)

    carried, outgoing = pl.pallas_call(
        dispatch_kernel,
        out_shape=(
            jax.ShapeDtypeStruct((ROWS_DEV, WIDTH), F32),
            jax.ShapeDtypeStruct((EXPERTS, CAP + EXTRA, WIDTH), BF16),
        ),
        in_specs=[VMEM] * 9,
        out_specs=(VMEM, VMEM),
        name="dispatch",
    )(
        msg_own,
        msg_far,
        msg_left,
        msg_right,
        decode_out,
        residual,
        gain,
        router_t,
        placing,
    )
    got = lax.all_to_all(outgoing, "exp", split_axis=0, concat_axis=0, tiled=True)
    got, up_other, down_other = lax.optimization_barrier((got, up_other, down_other))
    x, first, logits = pl.pallas_call(
        arrive_kernel,
        out_shape=(
            jax.ShapeDtypeStruct((CAP, D), BF16),
            jax.ShapeDtypeStruct((CAP, F1), BF16),
            jax.ShapeDtypeStruct((EXPERTS, ROWS_DEV), F32),
        ),
        in_specs=[SMEM, VMEM, VMEM],
        out_specs=(VMEM,) * 3,
        name="arrive",
    )(lax.axis_index("exp").reshape(1).astype(jnp.int32), got, placing32)

    first_z = across_z(first)
    x_left, x_right = along_y(x, 1), along_y(x, -1)
    first_z, x_left, x_right = lax.optimization_barrier((first_z, x_left, x_right))
    stack_z = across_z(jnp.concatenate([x[:, F1:], x_left[:, F1:], x_right[:, F1:]], axis=0))
    fz_left, fz_right = along_y(first_z, 1), along_y(first_z, -1)
    far_a, far_b = along_y(x_left[:, :HALF], 1), along_y(x_right[:, HALF:], -1)
    stack_z, fz_left, fz_right = lax.optimization_barrier((stack_z, fz_left, fz_right))
    far_z_a = along_y(fz_left[:, :HALF], 1)
    far_z_b = along_y(jnp.concatenate([fz_right[:, HALF:], stack_z[2 * CAP :]], axis=1), -1)
    pieces = (x, x_left, x_right, first_z, fz_left, fz_right, stack_z)
    pieces += (far_a, far_b, far_z_a, far_z_b)
    terms = expert_call(pieces, (gate_own, gate_other, up_own, up_other, down_own, down_other))

    own, left, right, far_a, far_b, own_z, left_z, right_z, far_z_a, far_z_b, stack, far_two = terms
    got_two = across_z(far_two)
    got_left, got_right = along_y(far_z_a, 1), along_y(far_z_b, -1)
    stack = across_z(stack)
    right_z = add(right_z, widen(got_left, 0, F1))
    left_z = add(left_z, widen(got_right, HALF1, F1))
    far_b = add(far_b, widen(got_two, F1 - HALF, HALF))
    z_left, z_right = along_y(right_z, 1), along_y(left_z, -1)
    got_a, got_b = along_y(far_a, 1), along_y(far_b, -1)
    z_left, z_right, got_a, got_b, stack = lax.optimization_barrier(
        (z_left, z_right, got_a, got_b, stack)
    )
    own_z = add(own_z, z_left, z_right)
    right = add(right, widen(got_a, 0, D), widen(stack[2 * CAP :], F1, D))
    left = add(left, widen(got_b, HALF, D), widen(stack[CAP : 2 * CAP], F1, D))
    got_left, got_right = along_y(right, 1), along_y(left, -1)
    got_z = across_z(own_z)
    result = add(own, got_left, got_right, widen(got_z, 0, D), widen(stack[:CAP], F1, D))
    result = result.reshape(CAP, EXPERTS, WIDTH).transpose(1, 0, 2)
    returned = lax.all_to_all(result, "exp", split_axis=0, concat_axis=0, tiled=True)

    onehot = expert_ids[:, :, None] == jnp.arange(EXPERTS, dtype=jnp.int32)[None, None, :]
    chosen = jnp.sum(jnp.where(onehot, logits.T[:, None, :], 0.0), axis=-1)
    route_weight = jax.nn.sigmoid(chosen - chosen[:, ::-1])
    mix_shape = jax.ShapeDtypeStruct((ROWS_DEV, SLOTS), BF16)
    mix_hi, mix_lo = pl.pallas_call(
        mixing_kernel,
        out_shape=(mix_shape, mix_shape),
        in_specs=[VMEM, VMEM],
        out_specs=(VMEM, VMEM),
        name="mixing",
    )(slot, route_weight)
    return pl.pallas_call(
        final_kernel,
        out_shape=jax.ShapeDtypeStruct((ROWS_DEV, WIDTH), BF16),
        in_specs=[VMEM] * 4,
        out_specs=VMEM,
        name="final",
    )(mix_hi, mix_lo, returned.reshape(SLOTS, WIDTH), carried)


def solution(mesh):
    placed = (
        P("ctx", "exp"),
        P(None, "ctx", "exp"),
        P(None, "ctx", "exp"),
        P("ctx", "exp"),
        P(None, "ctx", None, "exp"),
        P(None, "ctx", "exp"),
        P("ctx"),
        P("ctx", "exp"),
        P("exp"),
        P("exp", None),
        P("ctx", None),
        P(),
        P("exp", None, "ctx"),
        P("exp", None, "ctx"),
        P("exp", "ctx", None),
    )
    return jax.shard_map(
        on_device, mesh=mesh, in_specs=placed, out_specs=P("ctx", "exp"), check_vma=False
    )
```

```python
import functools

import jax
import jax.numpy as jnp
from jax import lax
from jax.experimental import pallas as pl
from jax.experimental.pallas import tpu as pltpu
from jax.sharding import PartitionSpec as P

D = 6144
HD = 128
QPK = 6
EXPERTS = 8
TOPK = 2
CAP = 40
FF_DEV = 512
SPAN_DEV = 128
ROWS_DEV = 144
N_Y = 4
WIDTH = D // EXPERTS
SLOTS = CAP * EXPERTS
MSG = QPK * HD + 128
EXTRA = 8

F1 = 4096
F2 = D - F1

NEG = -1e30
EPS = 1e-05
LOG2E = 1.4426950408889634
HEADS = 2
SCALE2 = HD ** (-0.5) * LOG2E
BF16 = jnp.bfloat16
F32 = jnp.float32
MIB = 2**20
VMEM = pl.BlockSpec(memory_space=pltpu.VMEM)
SMEM = pl.BlockSpec(memory_space=pltpu.SMEM)


def ctx_index(y, z, core):
    return y * 4 + z * 2 + core


def moved(value, place):
    pairs = []
    for y in range(N_Y):
        for z in range(2):
            for core in range(2):
                pairs.append((ctx_index(y, z, core), ctx_index(*place(y, z, core))))
    return lax.ppermute(value, "ctx", pairs)


def along_y(value, steps):
    return moved(value, lambda y, z, core: ((y + steps) % N_Y, z, core))


def across_z(value):
    return moved(value, lambda y, z, core: (y, 1 - z, core))


def across_core(value):
    return moved(value, lambda y, z, core: (y, z, 1 - core))


def dot_nt(a, b, precision=None):
    return lax.dot_general(
        a, b, (((1,), (1,)), ((), ())), preferred_element_type=F32, precision=precision
    )


def split3(value):
    hi = value.astype(BF16).astype(F32)
    rest = value - hi
    mid = rest.astype(BF16).astype(F32)
    return hi, mid, rest - mid


def flash_steps(place_ref, query, blocks):
    first = 1
    prompt = blocks[0].shape[1] - SPAN_DEV

    def scores_of(i):
        if i < len(blocks):
            return dot_nt(query, blocks[i][0, :prompt, :])
        keys = jnp.concatenate([block[0, prompt:, :] for block in blocks], axis=0)
        scores = dot_nt(query, keys)
        row = lax.broadcasted_iota(jnp.int32, scores.shape, 0) % SPAN_DEV
        col = lax.broadcasted_iota(jnp.int32, scores.shape, 1)
        block = col // SPAN_DEV
        source = jnp.full(scores.shape, place_ref[first], jnp.int32)
        for j in range(1, len(blocks)):
            source = jnp.where(block == j, place_ref[first + j], source)
        key = source * SPAN_DEV + col % SPAN_DEV
        return jnp.where(key <= row + place_ref[0] * SPAN_DEV, scores, NEG)

    def values_of(i):
        if i < len(blocks):
            values = blocks[i][1, :prompt, :]
        else:
            values = jnp.concatenate([block[1, prompt:, :] for block in blocks], axis=0)
        return jnp.concatenate([values, jnp.ones(values.shape, BF16)], axis=1)

    top = summed = None
    scores = scores_of(0)
    for i in range(len(blocks) + 1):
        following = scores_of(i + 1) if i < len(blocks) else None
        newest = jnp.max(scores, axis=1, keepdims=True)
        if top is not None:
            newest = jnp.maximum(top, newest)
        probs = jnp.exp2((scores - newest) * SCALE2).astype(BF16)
        part = jnp.dot(probs, values_of(i), preferred_element_type=F32)
        summed = part if top is None else summed * jnp.exp2((top - newest) * SCALE2) + part
        top, scores = newest, following
    return top, summed


def flash_all(place_ref, q_ref, b0, b1, b2, b3, msg_ref):
    lane = lax.broadcasted_iota(jnp.int32, (SPAN_DEV, 128), 1)

    def heads(t, stats):
        lanes = [
            pl.ds(pl.multiple_of((t * HEADS + j) * HD, HD), HD) for j in range(HEADS)
        ]
        query = jnp.concatenate([q_ref[:, at] for at in lanes], axis=0)
        top, summed = flash_steps(place_ref, query, (b0, b1, b2, b3))
        for j in range(HEADS):
            at = slice(j * SPAN_DEV, (j + 1) * SPAN_DEV)
            total = summed[at, HD:]
            msg_ref[:, lanes[j]] = (summed[at, :HD] / total).astype(BF16)
            for i, part in enumerate(split3(top[at] * SCALE2 + jnp.log2(total))):
                stats = jnp.where(lane == 3 * (t * HEADS + j) + i, part, stats)
        return stats

    stats = lax.fori_loop(0, QPK // HEADS, heads, jnp.zeros((SPAN_DEV, 128), F32))
    msg_ref[:, QPK * HD :] = stats.astype(BF16)


def flash_call(place, queries, blocks):
    rows = QPK * SPAN_DEV
    count = len(blocks) * blocks[0].shape[1]
    return pl.pallas_call(
        flash_all,
        out_shape=jax.ShapeDtypeStruct((SPAN_DEV, MSG), BF16),
        in_specs=[SMEM] + [VMEM] * (1 + len(blocks)),
        out_specs=VMEM,
        compiler_params=pltpu.CompilerParams(vmem_limit_bytes=20 * MIB),
        cost_estimate=pl.CostEstimate(
            flops=8 * rows * count * HD, bytes_accessed=4 * MIB, transcendentals=rows * count
        ),
        name="flash",
    )(place, queries, *blocks)


def dispatch_kernel(
    m0, m1, m2, m3, decode_ref, residual_ref, gain_ref, router_ref, placing_ref, carried_ref, out_ref
):
    msgs = (m0, m1, m2, m3)
    for h in range(QPK):
        lanes = slice(h * HD, (h + 1) * HD)
        levels = []
        for m in msgs:
            at = QPK * HD + 3 * h
            stat = m[:, at : at + 3].astype(F32)
            levels.append(stat[:, 0:1] + stat[:, 1:2] + stat[:, 2:3])
        top = functools.reduce(jnp.maximum, levels)
        weights = [jnp.exp2(level - top) for level in levels]
        total = sum(weights)
        summed = sum(w * m[:, lanes].astype(F32) for w, m in zip(weights, msgs))
        attn = (summed / total).astype(BF16).astype(F32)
        carried_ref[:SPAN_DEV, lanes] = residual_ref[:SPAN_DEV, lanes].astype(F32) + attn
    carried_ref[SPAN_DEV:, :] = residual_ref[SPAN_DEV:, :].astype(F32) + decode_ref[...].astype(F32)
    carried = carried_ref[...]
    gained = carried * gain_ref[...].astype(F32)
    logits = sum(dot_nt(router_ref[...], part.astype(BF16)) for part in split3(gained))
    ones = jnp.ones((EXTRA, WIDTH), BF16)
    squares = sum(dot_nt(ones, part.astype(BF16)) for part in split3(carried * carried))
    log_hi, log_mid, _ = split3(logits)
    sq_hi, sq_mid, _ = split3(squares)
    row = lax.broadcasted_iota(jnp.int32, squares.shape, 0)
    sq = jnp.where(row == 0, sq_hi, sq_mid)
    placed = jnp.dot(placing_ref[...], gained.astype(BF16), preferred_element_type=F32)
    for e in range(EXPERTS):
        out_ref[e, :CAP, :] = placed[e * CAP : (e + 1) * CAP, :].astype(BF16)
        out_ref[e, CAP:, :] = jnp.zeros((EXTRA, WIDTH), BF16)
        out_ref[e, CAP:, 0:ROWS_DEV] = log_hi.astype(BF16)
        out_ref[e, CAP:, 256 : 256 + ROWS_DEV] = log_mid.astype(BF16)
        out_ref[e, CAP:, 512 : 512 + ROWS_DEV] = sq.astype(BF16)


def arrive_kernel(expert_ref, got_ref, placing_ref, x_ref, first_ref, logits_ref):
    stats = got_ref[0, CAP:, :].astype(F32)
    for e in range(1, EXPERTS):
        stats = stats + got_ref[e, CAP:, :].astype(F32)
    logits = stats[:, 0:ROWS_DEV] + stats[:, 256 : 256 + ROWS_DEV]
    squares = stats[0:1, 512 : 512 + ROWS_DEV] + stats[1:2, 512 : 512 + ROWS_DEV]
    rscale = lax.rsqrt(squares / D + EPS)
    logits_ref[...] = logits * rscale
    placing = placing_ref[pl.ds(pl.multiple_of(expert_ref[0] * CAP, 8), CAP), :]
    scale = jnp.sum(placing * rscale, axis=1, keepdims=True)
    for e in range(EXPERTS):
        rows = (got_ref[e, :CAP, :].astype(F32) * scale).astype(BF16)
        begin = e * WIDTH
        end = begin + WIDTH
        x_ref[:, begin:end] = rows
        if begin < F1:
            first_ref[:, begin : min(end, F1)] = rows[:, : min(end, F1) - begin]


HALF = D // 2
HALF1 = F1 // 2
N_TILE = 256
DEPTH = D // 2
OUT_TILE = 1024
AHEAD = 6
N_SLOTS = 3
HBM = pl.BlockSpec(memory_space=pltpu.HBM)


def piece_places():
    places = [(0, 0, 0, D, 0, 0), (1, 0, 0, D, 0, 2), (2, 0, 0, D, 0, 4)]
    places += [(3, 0, 0, F1, 0, 1), (4, 0, 0, F1, 0, 3), (5, 0, 0, F1, 0, 5)]
    places += [(6, i * CAP, 0, F2, F1, 2 * i + 1) for i in range(3)]
    places += [(7, 0, 0, HALF, 0, 6), (8, 0, 0, HALF, HALF, 6)]
    places += [(9, 0, 0, HALF, 0, 7), (10, 0, 0, HALF, HALF, 7)]
    return places


N_PIECES = 11


def expert_kernel(*refs):
    pieces, weights = refs[:N_PIECES], refs[N_PIECES : N_PIECES + 6]
    outs, (x_ref, hidden_ref, gate_buf, down_buf, sems) = refs[N_PIECES + 6 : -5], refs[-5:]
    copies = []
    for i in range(2):
        for n in range(FF_DEV // N_TILE):
            for k in range(D // DEPTH):
                for w in range(2):
                    rows, cols = pl.ds(k * DEPTH, DEPTH), pl.ds(n * N_TILE, N_TILE)
                    slot = (i * 2 + n) % N_SLOTS * 2 + w
                    copies.append(
                        (weights[2 * w + i].at[0, rows, cols], gate_buf.at[slot, rows, :])
                    )
    for j in range(D // OUT_TILE):
        for i in range(2):
            cols = pl.ds(j * OUT_TILE, OUT_TILE)
            copies.append((weights[4 + i].at[0, :, cols], down_buf.at[i, :, cols]))
    copies = [pltpu.make_async_copy(src, dst, sems.at[i]) for i, (src, dst) in enumerate(copies)]
    for copy in copies[:AHEAD]:
        copy.start()
    done = 0

    def arrived():
        nonlocal done
        for _ in range(2):
            if done + AHEAD < len(copies):
                copies[done + AHEAD].start()
            copies[done].wait()
            done += 1

    for piece, top, begin, end, col, block in piece_places():
        x_ref[block * CAP : (block + 1) * CAP, col : col + end - begin] = pieces[piece][
            top : top + CAP, begin:end
        ]
    for tile in range(2 * FF_DEV // N_TILE):
        gate = up = None
        for k in range(D // DEPTH):
            arrived()
            at = slice(k * DEPTH, (k + 1) * DEPTH)
            x = x_ref[:, at]
            gate_k = jnp.dot(x, gate_buf[tile % N_SLOTS * 2, at, :], preferred_element_type=F32)
            up_k = jnp.dot(x, gate_buf[tile % N_SLOTS * 2 + 1, at, :], preferred_element_type=F32)
            gate = gate_k if gate is None else gate + gate_k
            up = up_k if up is None else up + up_k
        hidden = gate / (1.0 + jnp.exp(-gate)) * up
        hidden_ref[:, tile * N_TILE : (tile + 1) * N_TILE] = hidden.astype(BF16)

    own, left, right, far_a, far_b, own_z, left_z, right_z, far_z_a, far_z_b, stack, far_two = outs
    for j in range(D // OUT_TILE):
        arrived()
        begin = j * OUT_TILE
        at = slice(begin, begin + OUT_TILE)
        out = jnp.dot(hidden_ref[:, :FF_DEV], down_buf[0, :, at], preferred_element_type=F32)
        out = out + jnp.dot(hidden_ref[:, FF_DEV:], down_buf[1, :, at], preferred_element_type=F32)
        terms = [out[i * CAP : (i + 1) * CAP].astype(BF16) for i in range(8)]
        own[:, at], left[:, at], right[:, at] = terms[0], terms[2], terms[4]
        if begin < HALF:
            far_a[:, at] = terms[6]
        else:
            far_b[:, begin - HALF : begin - HALF + OUT_TILE] = terms[6]
        if begin < F1:
            own_z[:, at], left_z[:, at], right_z[:, at] = terms[1], terms[3], terms[5]
            if begin < HALF1:
                far_z_a[:, at] = terms[7]
            else:
                far_z_b[:, begin - HALF1 : begin - HALF1 + OUT_TILE] = terms[7]
        else:
            at = slice(begin - F1, begin - F1 + OUT_TILE)
            far_two[:, at] = terms[7]
            for i in range(3):
                stack[i * CAP : (i + 1) * CAP, at] = terms[2 * i + 1]


def rows_of(rows, width):
    return jax.ShapeDtypeStruct((rows, width), BF16)


def expert_call(pieces, weights):
    outs = (rows_of(CAP, D),) * 3 + (rows_of(CAP, HALF),) * 2
    outs += (rows_of(CAP, F1),) * 3 + (rows_of(CAP, HALF1),) * 2
    outs += (rows_of(3 * CAP, F2), rows_of(CAP, F2))
    n_copies = 2 * (FF_DEV // N_TILE) * (D // DEPTH) * 2 + 2 * (D // OUT_TILE)
    return pl.pallas_call(
        expert_kernel,
        out_shape=outs,
        in_specs=[VMEM] * N_PIECES + [HBM] * 6,
        out_specs=(VMEM,) * len(outs),
        scratch_shapes=[
            pltpu.VMEM((SLOTS, D), BF16),
            pltpu.VMEM((SLOTS, 2 * FF_DEV), BF16),
            pltpu.VMEM((2 * N_SLOTS, D, N_TILE), BF16),
            pltpu.VMEM((2, FF_DEV, D), BF16),
            pltpu.SemaphoreType.DMA((n_copies,)),
        ],
        compiler_params=pltpu.CompilerParams(vmem_limit_bytes=42 * MIB),
        cost_estimate=pl.CostEstimate(
            flops=2 * SLOTS * D * 6 * FF_DEV, bytes_accessed=44 * MIB, transcendentals=0
        ),
        name="experts",
    )(*pieces, *weights)


def add(*values):
    return functools.reduce(jnp.add, [v.astype(F32) for v in values]).astype(BF16)


def widen(value, begin, width):
    return jnp.pad(value, ((0, 0), (begin, width - begin - value.shape[1])))


def final_kernel(hi_ref, lo_ref, got_ref, carried_ref, out_ref):
    got = got_ref[...]
    moe = jnp.dot(hi_ref[...], got, preferred_element_type=F32)
    moe = moe + jnp.dot(lo_ref[...], got, preferred_element_type=F32)
    out_ref[...] = (carried_ref[...] + moe).astype(BF16)


def mixing_kernel(slot_ref, weight_ref, hi_ref, lo_ref):
    lane = lax.broadcasted_iota(jnp.int32, (ROWS_DEV, SLOTS), 1)
    mix = jnp.zeros((ROWS_DEV, SLOTS), F32)
    for k in range(TOPK):
        mix = jnp.where(slot_ref[:, k : k + 1] == lane, weight_ref[:, k : k + 1], mix)
    hi = mix.astype(BF16)
    hi_ref[...] = hi
    lo_ref[...] = (mix - hi.astype(F32)).astype(BF16)


def decode_kernel(len_ref, q_ref, cache_ref, new_ref, out_ref):
    count, length = cache_ref.shape[1], cache_ref.shape[2]
    rows = QPK * count
    query = jnp.concatenate([q_ref[:, h * HD : (h + 1) * HD] for h in range(QPK)], axis=0)
    row = lax.broadcasted_iota(jnp.int32, (rows, 1), 0) % count
    scores = jnp.zeros((rows, length), F32)
    lengths = jnp.zeros((rows, 1), jnp.int32)
    for r in range(count):
        scores = jnp.where(row == r, dot_nt(query, cache_ref[0, r]), scores)
        lengths = jnp.where(row == r, len_ref[r], lengths)
    key = jnp.concatenate([new_ref[0].astype(F32)] * QPK, axis=0)
    value = jnp.concatenate([new_ref[1].astype(F32)] * QPK, axis=0)
    own = jnp.sum(query.astype(F32) * key, axis=1, keepdims=True)
    live = lax.broadcasted_iota(jnp.int32, (rows, length), 1) < lengths
    top = jnp.maximum(jnp.max(jnp.where(live, scores, NEG), axis=1, keepdims=True), own)
    weights = jnp.where(live, jnp.exp2((scores - top) * SCALE2), 0.0)
    own_weight = jnp.exp2((own - top) * SCALE2)
    total = jnp.sum(weights, axis=1, keepdims=True) + own_weight
    summed = own_weight.astype(BF16).astype(F32) * value
    for r in range(count):
        probs = jnp.where(row == r, weights, 0.0).astype(BF16)
        summed = summed + jnp.dot(probs, cache_ref[1, r], preferred_element_type=F32)
    result = (summed / total).astype(BF16)
    for h in range(QPK):
        out_ref[:, h * HD : (h + 1) * HD] = result[h * count : (h + 1) * count]


def slots_kernel(capacity_ref, ids_ref, slot_ref, placing_ref, placing32_ref):
    lane = lax.broadcasted_iota(jnp.int32, (ROWS_DEV, 128), 1)
    ids = [ids_ref[:, k : k + 1] for k in range(TOPK)]
    named = [(lane == i).astype(F32) for i in ids]
    square = (ROWS_DEV, ROWS_DEV)
    earlier = lax.broadcasted_iota(jnp.int32, square, 0) > lax.broadcasted_iota(jnp.int32, square, 1)
    prior = jnp.dot(
        earlier.astype(F32).astype(BF16),
        (named[0] + named[1]).astype(BF16),
        preferred_element_type=F32,
    )
    limits = jnp.zeros((ROWS_DEV, 128), F32)
    for e in range(EXPERTS):
        limits = jnp.where(lane == e, capacity_ref[e].astype(F32), limits)
    wide = lax.broadcasted_iota(jnp.int32, (ROWS_DEV, 384), 1)
    placing = jnp.zeros((ROWS_DEV, 384), F32)
    for k in range(TOPK):
        position = jnp.sum(prior * named[k], axis=1, keepdims=True)
        limit = jnp.sum(limits * named[k], axis=1, keepdims=True)
        prior = prior + named[k]
        slot = jnp.where(position < limit, ids[k] * CAP + position.astype(jnp.int32), -1)
        slot_ref[:, k : k + 1] = slot
        placing = jnp.where(wide == slot, 1.0, placing)
    shape = (SLOTS, 384)
    same = lax.broadcasted_iota(jnp.int32, shape, 0) == lax.broadcasted_iota(jnp.int32, shape, 1)
    turned = dot_nt(same.astype(F32).astype(BF16), placing.astype(BF16))
    placing_ref[...] = turned.astype(BF16)
    placing32_ref[...] = turned


def on_device(
    span_q,
    prompt_kv,
    span_kv,
    decode_q,
    decode_cache,
    decode_new,
    decode_len,
    residual,
    norm_gain,
    router,
    expert_ids,
    capacity,
    w_gate,
    w_up,
    w_down,
):
    here = lax.axis_index("ctx")
    y, z, core = here // 4, (here // 2) % 2, here % 2
    kv = jnp.concatenate([prompt_kv, span_kv], axis=1)
    kv_z = across_z(kv)
    kv_core = across_core(kv)
    q_left, q_right = along_y(span_q, 1), along_y(span_q, -1)
    gate_own, gate_other = w_gate, across_core(w_gate)
    sources = [
        ctx_index(y, a, b) for a, b in ((z, core), (z, 1 - core), (1 - z, core), (1 - z, 1 - core))
    ]
    places = [
        jnp.stack([ctx_index((y + steps) % N_Y, z, core)] + sources).astype(jnp.int32)
        for steps in (-1, 1, 2, 0)
    ]
    decode_out = pl.pallas_call(
        decode_kernel,
        out_shape=jax.ShapeDtypeStruct(decode_q.shape, BF16),
        in_specs=[SMEM] + [VMEM] * 3,
        out_specs=VMEM,
        name="decode",
    )(decode_len, decode_q, decode_cache, decode_new)
    slot, placing, placing32 = pl.pallas_call(
        slots_kernel,
        out_shape=(
            jax.ShapeDtypeStruct((ROWS_DEV, TOPK), jnp.int32),
            jax.ShapeDtypeStruct((SLOTS, ROWS_DEV), BF16),
            jax.ShapeDtypeStruct((SLOTS, ROWS_DEV), F32),
        ),
        in_specs=[SMEM, VMEM],
        out_specs=(VMEM,) * 3,
        name="slots",
    )(capacity, expert_ids)
    gain = norm_gain.reshape(1, WIDTH)
    router_t = router.T
    q_left, decode_out, slot = lax.optimization_barrier((q_left, decode_out, slot))
    q_far = along_y(q_left, 1)
    waited = (kv_core, kv_z, q_left, q_right, q_far, gate_other, decode_out, gain, router_t)
    waited, places, weights, slots = lax.optimization_barrier(
        (waited, places, (w_up, w_down), (slot, placing, placing32))
    )
    kv_core, kv_z, q_left, q_right, q_far, gate_other, decode_out, gain, router_t = waited
    slot, placing, placing32 = slots
    kv_zc = across_core(kv_z)
    kv_zc, weights = lax.optimization_barrier((kv_zc, weights))
    up_own, down_own = weights
    up_other, down_other = [across_core(w) for w in weights]
    blocks = (kv, kv_core, kv_z, kv_zc)
    part_far = flash_call(places[2], q_far, blocks)
    msg_far = along_y(part_far, 2)
    part_left = flash_call(places[0], q_left, blocks)
    msg_right = along_y(part_left, -1)
    q_right, part_far, part_left = lax.optimization_barrier((q_right, part_far, part_left))
    msg_left = along_y(flash_call(places[1], q_right, blocks), 1)
    msg_own = flash_call(places[3], span_q, blocks)

    carried, outgoing = pl.pallas_call(
        dispatch_kernel,
        out_shape=(
            jax.ShapeDtypeStruct((ROWS_DEV, WIDTH), F32),
            jax.ShapeDtypeStruct((EXPERTS, CAP + EXTRA, WIDTH), BF16),
        ),
        in_specs=[VMEM] * 9,
        out_specs=(VMEM, VMEM),
        name="dispatch",
    )(
        msg_own,
        msg_far,
        msg_left,
        msg_right,
        decode_out,
        residual,
        gain,
        router_t,
        placing,
    )
    got = lax.all_to_all(outgoing, "exp", split_axis=0, concat_axis=0, tiled=True)
    got, up_other, down_other = lax.optimization_barrier((got, up_other, down_other))
    x, first, logits = pl.pallas_call(
        arrive_kernel,
        out_shape=(
            jax.ShapeDtypeStruct((CAP, D), BF16),
            jax.ShapeDtypeStruct((CAP, F1), BF16),
            jax.ShapeDtypeStruct((EXPERTS, ROWS_DEV), F32),
        ),
        in_specs=[SMEM, VMEM, VMEM],
        out_specs=(VMEM,) * 3,
        name="arrive",
    )(lax.axis_index("exp").reshape(1).astype(jnp.int32), got, placing32)

    first_z = across_z(first)
    x_left, x_right = along_y(x, 1), along_y(x, -1)
    first_z, x_left, x_right = lax.optimization_barrier((first_z, x_left, x_right))
    stack_z = across_z(jnp.concatenate([x[:, F1:], x_left[:, F1:], x_right[:, F1:]], axis=0))
    fz_left, fz_right = along_y(first_z, 1), along_y(first_z, -1)
    far_a, far_b = along_y(x_left[:, :HALF], 1), along_y(x_right[:, HALF:], -1)
    stack_z, fz_left, fz_right = lax.optimization_barrier((stack_z, fz_left, fz_right))
    far_z_a = along_y(fz_left[:, :HALF], 1)
    far_z_b = along_y(jnp.concatenate([fz_right[:, HALF:], stack_z[2 * CAP :]], axis=1), -1)
    pieces = (x, x_left, x_right, first_z, fz_left, fz_right, stack_z)
    pieces += (far_a, far_b, far_z_a, far_z_b)
    terms = expert_call(pieces, (gate_own, gate_other, up_own, up_other, down_own, down_other))

    own, left, right, far_a, far_b, own_z, left_z, right_z, far_z_a, far_z_b, stack, far_two = terms
    got_two = across_z(far_two)
    got_left, got_right = along_y(far_z_a, 1), along_y(far_z_b, -1)
    stack = across_z(stack)
    right_z = add(right_z, widen(got_left, 0, F1))
    left_z = add(left_z, widen(got_right, HALF1, F1))
    far_b = add(far_b, widen(got_two, F1 - HALF, HALF))
    z_left, z_right = along_y(right_z, 1), along_y(left_z, -1)
    got_a, got_b = along_y(far_a, 1), along_y(far_b, -1)
    z_left, z_right, got_a, got_b, stack = lax.optimization_barrier(
        (z_left, z_right, got_a, got_b, stack)
    )
    own_z = add(own_z, z_left, z_right)
    right = add(right, widen(got_a, 0, D), widen(stack[2 * CAP :], F1, D))
    left = add(left, widen(got_b, HALF, D), widen(stack[CAP : 2 * CAP], F1, D))
    got_left, got_right = along_y(right, 1), along_y(left, -1)
    got_z = across_z(own_z)
    result = add(own, got_left, got_right, widen(got_z, 0, D), widen(stack[:CAP], F1, D))
    result = result.reshape(CAP, EXPERTS, WIDTH).transpose(1, 0, 2)
    returned = lax.all_to_all(result, "exp", split_axis=0, concat_axis=0, tiled=True)

    onehot = expert_ids[:, :, None] == jnp.arange(EXPERTS, dtype=jnp.int32)[None, None, :]
    chosen = jnp.sum(jnp.where(onehot, logits.T[:, None, :], 0.0), axis=-1)
    route_weight = jax.nn.sigmoid(chosen - chosen[:, ::-1])
    mix_shape = jax.ShapeDtypeStruct((ROWS_DEV, SLOTS), BF16)
    mix_hi, mix_lo = pl.pallas_call(
        mixing_kernel,
        out_shape=(mix_shape, mix_shape),
        in_specs=[VMEM, VMEM],
        out_specs=(VMEM, VMEM),
        name="mixing",
    )(slot, route_weight)
    return pl.pallas_call(
        final_kernel,
        out_shape=jax.ShapeDtypeStruct((ROWS_DEV, WIDTH), BF16),
        in_specs=[VMEM] * 4,
        out_specs=VMEM,
        name="final",
    )(mix_hi, mix_lo, returned.reshape(SLOTS, WIDTH), carried)


def solution(mesh):
    placed = (
        P("ctx", "exp"),
        P(None, "ctx", "exp"),
        P(None, "ctx", "exp"),
        P("ctx", "exp"),
        P(None, "ctx", None, "exp"),
        P(None, "ctx", "exp"),
        P("ctx"),
        P("ctx", "exp"),
        P("exp"),
        P("exp", None),
        P("ctx", None),
        P(),
        P("exp", None, "ctx"),
        P("exp", None, "ctx"),
        P("exp", "ctx", None),
    )
    return jax.shard_map(
        on_device, mesh=mesh, in_specs=placed, out_specs=P("ctx", "exp"), check_vma=False
    )
```
